256 devices in a mesh: lat: 16 (over x_lo, y, core), lon: 16 (over x_hi, z).
Axes of the slice: x: 4 (x_hi: 2, x_lo: 2; x = x_hi * 2 + x_lo), y: 4, z: 8, core: 2. Of those that a mesh axis runs over, the one named last changes fastest.
Arguments:
- out_first: float32 [2, 192, 384, 192], P(None, 'lat', 'lon'), may hold values from -6 to 6
- out_second: float32 [2, 192, 384, 192], P(None, 'lat', 'lon'), may hold values from -6 to 6
- cot_first: bfloat16 [2, 192, 384, 192], P(None, 'lat', 'lon'), may hold values from -6 to 6
- cot_second: bfloat16 [2, 192, 384, 192], P(None, 'lat', 'lon'), may hold values from -6 to 6
- gain_attn: float32 [192], replicated, may hold values from 0.5 to 1.5
- w_qkv: bfloat16 [192, 576], replicated, may hold values from -0.4375 to 0.4375
- w_proj: bfloat16 [192, 192], replicated, may hold values from -0.4375 to 0.4375
- earth_bias: bfloat16 [32, 1, 6, 144, 144], P('lat'), may hold values from -3 to 303
- gain_mlp: float32 [192], replicated, may hold values from 0.5 to 1.5
- w_up: bfloat16 [192, 768], replicated, may hold values from -0.4375 to 0.4375
- w_down: bfloat16 [768, 192], replicated, may hold values from -0.21875 to 0.21875
Outputs:
- in_first: float32 [2, 192, 384, 192], P(None, 'lat', 'lon')
- in_second: float32 [2, 192, 384, 192], P(None, 'lat', 'lon')
- grad_first: float32 [2, 192, 384, 192], P(None, 'lat', 'lon')
- grad_second: float32 [2, 192, 384, 192], P(None, 'lat', 'lon')
- grad_gain_attn: float32 [192], replicated
- grad_qkv: float32 [192, 576], replicated
- grad_proj: float32 [192, 192], replicated
- grad_bias: float32 [32, 1, 6, 144, 144], P('lat')
- grad_gain_mlp: float32 [192], replicated
- grad_up: float32 [192, 768], replicated
- grad_down: float32 [768, 192], replicated
The draws below stay inside these ranges and needn't reach their ends.
All inputs are finite; a program needn't handle non-finite values.
Results may differ from the reference program's by a relative error of at most 0.0099.
Values sent between devices are 32-bit elements; how exact they have to be, the bound alone decides.
No kernel may reach another device: no remote copies, remote signals or barrier semaphores. Data moves between devices by JAX's collectives and lax.ppermute only.
A program may use at most 64 MiB of HBM per device.

```python
import jax
import jax.numpy as jnp
from jax import lax

D = 192
HEADS = 6
HEAD_DIM = 32
FF = 768
WIN_LEV = 2
WIN_LAT = 6
WIN_LON = 12
LEV = 2
NA = 192
NO = 384
NWA = 32
NWL = 1
WIN = 144


def draw_earth_bias(key, part):
    key = jax.random.fold_in(key, 11)
    table_shape = (NWA, NWL, HEADS, WIN, WIN)
    baseline = jnp.clip(0.5 * jax.random.normal(key, table_shape, jnp.float32), -3.0, 3.0)
    return baseline.astype(jnp.bfloat16)


def level_of(key, dims, cuts, least, high):
    gain, own = 1.0, jax.random.fold_in(key, 6)
    for dim, parts in cuts:
        heights = jnp.exp(jax.random.uniform(jax.random.fold_in(own, dim), (parts,), jnp.float32, least / len(cuts), high / len(cuts)))
        gain = gain * jnp.repeat(heights, dims[dim] // parts).reshape([-1 if axis == dim else 1 for axis in range(len(dims))])
    return gain


def scatter_about(rng, shape, width, bound, split=(), dtype=jnp.bfloat16):
    drawn = jax.random.normal(rng, shape, jnp.float32) * width
    if len(split) > 0:
        drawn = level_of(rng, shape, split, -0.22, 0.18) * drawn
    return jnp.clip(drawn, min=-bound, max=bound).astype(dtype)


def setup_inputs(seed: int = 0) -> dict:
    seeds = jax.random.split(jax.random.key(seed), 12)
    out_first = scatter_about(seeds[0], (LEV, NA, NO, D), 1.0, 6.0, ((1, 16), (2, 16)), jnp.float32)
    out_second = scatter_about(seeds[1], (LEV, NA, NO, D), 1.0, 6.0, ((1, 16), (2, 16)), jnp.float32)
    cot_first = scatter_about(seeds[2], (LEV, NA, NO, D), 1.0, 6.0, ((1, 16), (2, 16)))
    cot_second = scatter_about(seeds[3], (LEV, NA, NO, D), 1.0, 6.0, ((1, 16), (2, 16)))
    gain_attn = jnp.clip(1.0 + 0.1 * jax.random.normal(seeds[4], (D,), jnp.float32), 0.5, 1.5)
    w_qkv = scatter_about(seeds[5], (D, 3 * D), D ** -0.5, 0.4375)
    w_proj = scatter_about(seeds[6], (D, D), D ** -0.5, 0.4375)
    earth_bias = draw_earth_bias(jax.random.fold_in(seeds[11], 71), 0)
    gain_mlp = jnp.clip(1.0 + 0.1 * jax.random.normal(seeds[8], (D,), jnp.float32), 0.5, 1.5)
    w_up = scatter_about(seeds[9], (D, FF), D ** -0.5, 0.4375)
    w_down = scatter_about(seeds[10], (FF, D), FF ** -0.5, 0.21875)
    return {"out_first": out_first, "out_second": out_second, "cot_first": cot_first, "cot_second": cot_second, "gain_attn": gain_attn, "w_qkv": w_qkv, "w_proj": w_proj, "earth_bias": earth_bias, "gain_mlp": gain_mlp, "w_up": w_up, "w_down": w_down}


norm_eps = 1e-05
gelu_scale = 0.7978845608028654
gelu_cubic = 0.044715
masked_score = -1000000000.0

def widen(array):
    return array.astype(jnp.float32)

def norm_parts(field):
    average = lax.optimization_barrier(jnp.mean(field, -1, keepdims=True))
    centred = field - average
    inverse = lax.rsqrt(lax.optimization_barrier(jnp.mean(centred * centred, -1, keepdims=True)) + norm_eps)
    return (centred * inverse, inverse)

def norm_back(cot_normed, norm_gain, unit_field, inverse):
    cot_unit = cot_normed * norm_gain
    return inverse * (cot_unit - lax.optimization_barrier(jnp.mean(cot_unit, -1, keepdims=True)) - unit_field * lax.optimization_barrier(jnp.mean(cot_unit * unit_field, -1, keepdims=True)))

def feedforward_pass(tokens, cot_branch, norm_gain, w_up, w_down):
    unit_field, inverse = norm_parts(tokens)
    normed = (unit_field * norm_gain).astype(jnp.bfloat16)
    up_proj = jnp.dot(normed, w_up, preferred_element_type=jnp.float32)
    tanh_val = jnp.tanh(gelu_scale * (up_proj + gelu_cubic * up_proj * up_proj * up_proj))
    hidden = (0.5 * up_proj * (1.0 + tanh_val)).astype(jnp.bfloat16)
    branch = jnp.dot(hidden, w_down, preferred_element_type=jnp.float32)
    grad_down = jnp.dot(hidden.T, cot_branch, preferred_element_type=jnp.float32)
    cot_hidden = jnp.dot(cot_branch, w_down.T, preferred_element_type=jnp.float32)
    slope = 0.5 * (1.0 + tanh_val) + 0.5 * up_proj * (1.0 - tanh_val * tanh_val) * gelu_scale * (1.0 + 3.0 * gelu_cubic * up_proj * up_proj)
    cot_up = (cot_hidden * slope).astype(jnp.bfloat16)
    grad_up = jnp.dot(normed.T, cot_up, preferred_element_type=jnp.float32)
    cot_normed = jnp.dot(cot_up, w_up.T, preferred_element_type=jnp.float32)
    grad_gain = lax.optimization_barrier(jnp.sum(cot_normed * unit_field, 0))
    cot_tokens = norm_back(cot_normed, norm_gain, unit_field, inverse)
    return (branch, cot_tokens, grad_gain, grad_up, grad_down)

def group_codes(window_rows, total_lat, levels):
    position = jnp.arange(WIN_LEV * WIN_LAT * WIN_LON).astype(jnp.int32)
    level_pos = position // (WIN_LAT * WIN_LON)
    lat_pos = position // WIN_LON % WIN_LAT
    level_roll = jnp.arange(levels // WIN_LEV).astype(jnp.int32)[:, None] * WIN_LEV + level_pos[None, :]
    level_group = ((level_roll - WIN_LEV // 2) % levels + WIN_LEV // 2) // WIN_LEV
    lat_roll = window_rows[:, None] * WIN_LAT + lat_pos[None, :]
    lat_group = ((lat_roll - WIN_LAT // 2) % total_lat + WIN_LAT // 2) // WIN_LAT
    return level_group[None, :, :] * (total_lat + 1) + lat_group[:, None, :]

def into_windows(field):
    levels, lat_rows, columns, channels = field.shape
    shaped = field.reshape(levels // WIN_LEV, WIN_LEV, lat_rows // WIN_LAT, WIN_LAT, columns // WIN_LON, WIN_LON, channels)
    shaped = shaped.transpose(2, 0, 4, 1, 3, 5, 6)
    return shaped.reshape(lat_rows // WIN_LAT, levels // WIN_LEV, columns // WIN_LON, WIN_LEV * WIN_LAT * WIN_LON, channels)

def from_windows(windows):
    bands, groups, sectors, cells, channels = windows.shape
    shaped = windows.reshape(bands, groups, sectors, WIN_LEV, WIN_LAT, WIN_LON, channels)
    shaped = shaped.transpose(1, 3, 0, 4, 2, 5, 6)
    return shaped.reshape(groups * WIN_LEV, bands * WIN_LAT, sectors * WIN_LON, channels)

def attention_pass(windows, cot_windows, bias_table, group_code, norm_gain, w_qkv, w_proj):
    unit_field, inverse = norm_parts(windows)
    normed = (unit_field * norm_gain).astype(jnp.bfloat16)
    qkv = jnp.einsum('blowc,ce->blowe', widen(normed), widen(w_qkv)).astype(jnp.bfloat16)
    split_qkv = qkv.reshape(qkv.shape[:4] + (3, HEADS, HEAD_DIM))
    queries = widen(split_qkv[..., 0, :, :])
    key_part = widen(split_qkv[..., 1, :, :])
    value_part = widen(split_qkv[..., 2, :, :])
    score_scale = HEAD_DIM ** (-0.5)
    scores = jnp.einsum('blowhe,blovhe->blohwv', queries, key_part) * score_scale + widen(bias_table)[:, :, None]
    same_group = group_code[:, :, None, None, :, None] == group_code[:, :, None, None, None, :]
    scores = jnp.where(same_group, scores, masked_score)
    row_max = lax.optimization_barrier(jnp.max(scores, -1, keepdims=True))
    exponent = jnp.exp(scores - row_max)
    probability = exponent / lax.optimization_barrier(jnp.sum(exponent, -1, keepdims=True))
    weights = probability.astype(jnp.bfloat16)
    attended = jnp.einsum('blohwv,blovhe->blowhe', widen(weights), value_part).astype(jnp.bfloat16)
    attended = attended.reshape(qkv.shape[:4] + (HEADS * HEAD_DIM,))
    branch = jnp.einsum('blowc,cd->blowd', widen(attended), widen(w_proj))
    cot_low = cot_windows.astype(jnp.bfloat16)
    grad_proj = jnp.einsum('blowc,blowd->cd', widen(attended), widen(cot_low))
    cot_attended = jnp.einsum('blowd,cd->blowc', widen(cot_low), widen(w_proj)).astype(jnp.bfloat16)
    cot_attended = cot_attended.reshape(queries.shape)
    cot_weights = jnp.einsum('blowhe,blovhe->blohwv', widen(cot_attended), value_part)
    cot_value = jnp.einsum('blohwv,blowhe->blovhe', widen(weights), widen(cot_attended))
    cot_scores = probability * (cot_weights - lax.optimization_barrier(jnp.sum(cot_weights * probability, -1, keepdims=True)))
    grad_bias = lax.optimization_barrier(jnp.sum(cot_scores, 2))
    cot_scaled = (cot_scores * score_scale).astype(jnp.bfloat16)
    cot_query = jnp.einsum('blohwv,blovhe->blowhe', widen(cot_scaled), key_part)
    cot_key = jnp.einsum('blohwv,blowhe->blovhe', widen(cot_scaled), queries)
    cot_qkv = jnp.stack([cot_query, cot_key, cot_value], -3).reshape(qkv.shape).astype(jnp.bfloat16)
    grad_qkv = jnp.einsum('blowc,blowe->ce', widen(normed), widen(cot_qkv))
    cot_normed = jnp.einsum('blowe,ce->blowc', widen(cot_qkv), widen(w_qkv))
    grad_gain = lax.optimization_barrier(jnp.sum(cot_normed * unit_field, (0, 1, 2, 3)))
    cot_inputs = norm_back(cot_normed, norm_gain, unit_field, inverse)
    return (branch, cot_inputs, grad_gain, grad_qkv, grad_proj, grad_bias)

def reference(out_first, out_second, cot_first, cot_second, gain_attn, w_qkv, w_proj, earth_bias, gain_mlp, w_up, w_down):

    def level_step(sums_so_far, level_block):
        tokens, cot_level = level_block
        results = feedforward_pass(tokens.reshape(-1, D), cot_level.reshape(-1, D), gain_mlp, w_up, w_down)
        branch, cot_tokens, grad_gain, grad_up, grad_down = results
        totals = (sums_so_far[0] + grad_gain, sums_so_far[1] + grad_up, sums_so_far[2] + grad_down)
        return (totals, (branch.reshape(tokens.shape), cot_tokens.reshape(tokens.shape)))
    start_mlp = (jnp.zeros((D,), jnp.float32), jnp.zeros((D, FF), jnp.float32), jnp.zeros((FF, D), jnp.float32))
    mlp_sums, mlp_outs = lax.scan(level_step, start_mlp, (out_first, cot_second))
    mlp_branch, cot_mlp = mlp_outs
    in_second = out_second - mlp_branch
    grad_first = widen(cot_first) + cot_mlp
    shifts = (WIN_LEV // 2, WIN_LAT // 2, WIN_LON // 2)
    back_shifts = (-(WIN_LEV // 2), -(WIN_LAT // 2), -(WIN_LON // 2))
    rolled = into_windows(jnp.roll(in_second, shifts, axis=(0, 1, 2)))
    cot_rolled = into_windows(jnp.roll(grad_first, shifts, axis=(0, 1, 2)))
    group_code = group_codes(jnp.arange(NWA).astype(jnp.int32), NA, LEV)

    def band_step(sums_so_far, band):
        windows, cot_windows, bias_table, band_code = band
        results = attention_pass(windows[None], cot_windows[None], bias_table[None], band_code[None], gain_attn, w_qkv, w_proj)
        branch, cot_inputs, grad_gain, grad_qkv, grad_proj, grad_bias = results
        totals = (sums_so_far[0] + grad_gain, sums_so_far[1] + grad_qkv, sums_so_far[2] + grad_proj)
        return (totals, (branch[0], cot_inputs[0], grad_bias[0]))
    start_attn = (jnp.zeros((D,), jnp.float32), jnp.zeros((D, 3 * D), jnp.float32), jnp.zeros((D, D), jnp.float32))
    attn_sums, attn_outs = lax.scan(band_step, start_attn, (rolled, cot_rolled, earth_bias, group_code))
    attn_branch, cot_attn, grad_bias = attn_outs
    in_first = out_first - jnp.roll(from_windows(attn_branch), back_shifts, axis=(0, 1, 2))
    grad_second = widen(cot_second) + jnp.roll(from_windows(cot_attn), back_shifts, axis=(0, 1, 2))
    return (in_first, in_second, grad_first, grad_second, attn_sums[0], attn_sums[1], attn_sums[2], grad_bias, mlp_sums[0], mlp_sums[1], mlp_sums[2])
```

```python
import functools

import jax
import jax.numpy as jnp
from jax import lax
from jax.experimental import pallas as pl
from jax.experimental.pallas import tpu as pltpu
from jax.sharding import PartitionSpec as P

HEADS = 6
HEAD_DIM = 32
D = 192
FF = 768
LEV = 2
WIN_LAT = 6
WIN_LON = 12
CELLS = WIN_LAT * WIN_LON
BANDS = 2
SECTORS = 2
ROWS = BANDS * WIN_LAT
COLS = SECTORS * WIN_LON
TOKENS = LEV * ROWS * COLS
HALF_LAT = WIN_LAT // 2
HALF_LON = WIN_LON // 2
STACK = HEADS * CELLS
LANES = 128

norm_eps = 1e-05
gelu_scale = 0.7978845608028654
gelu_cubic = 0.044715
masked_score = -1000000000.0
padded_score = -1e30
score_scale = HEAD_DIM ** (-0.5)

f32 = jnp.float32
bf16 = jnp.bfloat16


def nn(a, b):
    return lax.dot_general(a, b, (((1,), (0,)), ((), ())), preferred_element_type=f32)


def nt(a, b):
    return lax.dot_general(a, b, (((1,), (1,)), ((), ())), preferred_element_type=f32)


def tn(a, b):
    return lax.dot_general(a, b, (((0,), (0,)), ((), ())), preferred_element_type=f32)


def norm_parts(field):
    average = jnp.mean(field, -1, keepdims=True)
    centred = field - average
    inverse = lax.rsqrt(jnp.mean(centred * centred, -1, keepdims=True) + norm_eps)
    return (centred * inverse, inverse)


def norm_back(cot_normed, norm_gain, unit_field, inverse):
    cot_unit = cot_normed * norm_gain
    return inverse * (
        cot_unit
        - jnp.mean(cot_unit, -1, keepdims=True)
        - unit_field * jnp.mean(cot_unit * unit_field, -1, keepdims=True)
    )


def two_halves(first, second, keep_ref, send_ref, where):
    mine = lax.rem(lax.axis_index("lat"), 2) == 0
    keep_ref[where] = jnp.where(mine, first, second)
    send_ref[where] = jnp.where(mine, second, first)


def lat_row(array, level, row):
    return ((array * LEV + level) * HALF_LAT + row) * (COLS - HALF_LON)


def lon_row(array, level, row):
    return ((array * LEV + level) * (ROWS - HALF_LAT) + row) * HALF_LON


def cor_row(array, level, row):
    return ((array * LEV + level) * HALF_LAT + row) * HALF_LON


LAT_ROWS = lat_row(2, 0, 0)
LON_ROWS = lon_row(2, 0, 0)
COR_ROWS = cor_row(2, 0, 0)
KEEP_R = ROWS - HALF_LAT
KEEP_C = COLS - HALF_LON


def ff_kernel(
    first_ref, second_ref, cot_first_ref, cot_second_ref, gain_ref, up_ref, down_ref,
    in_second_ref, grad_first_ref, lat_ref, lon_ref, cor_ref, keep_ref, send_ref, gain_out_ref,
    hidden_ref, cot_up_ref, normed_ref,
):
    tokens = first_ref[...].reshape(TOKENS, D)
    gain = gain_ref[...]
    unit_field, inverse = norm_parts(tokens)
    normed_ref[...] = (unit_field * gain).astype(bf16)
    cot = cot_second_ref[...].astype(f32).reshape(TOKENS, D).astype(bf16)
    w_up = up_ref[...]
    w_down = down_ref[...]
    step = 96
    for i in range(TOKENS // step):
        part = pl.ds(i * step, step)
        up_proj = nn(normed_ref[part, :], w_up)
        square = up_proj * up_proj
        half = 0.5 * (1.0 + jnp.tanh(up_proj * (gelu_scale + gelu_scale * gelu_cubic * square)))
        hidden_ref[part, :] = (up_proj * half).astype(bf16)
        cot_hidden = nt(cot[i * step : (i + 1) * step], w_down)
        slope = half + (half * (1.0 - half)) * up_proj * (
            2.0 * gelu_scale + 6.0 * gelu_scale * gelu_cubic * square
        )
        cot_up_ref[part, :] = (cot_hidden * slope).astype(bf16)
    hidden = hidden_ref[...]
    cot_up = cot_up_ref[...]
    shape = (LEV, ROWS, COLS, D)
    in_second_ref[...] = second_ref[...] - nn(hidden, w_down).reshape(shape)
    cot_normed = nt(cot_up, w_up)
    gain_out_ref[...] = jnp.sum(cot_normed * unit_field, 0, keepdims=True)
    back = norm_back(cot_normed, gain, unit_field, inverse)
    grad_first_ref[...] = cot_first_ref[...].astype(f32) + back.reshape(shape)
    for array, ref in enumerate((in_second_ref, grad_first_ref)):
        for level in range(LEV):
            for row in range(HALF_LAT):
                at = lat_row(array, level, row)
                lat_ref[at : at + KEEP_C, :] = ref[level, KEEP_R + row, 0:KEEP_C, :]
                at = cor_row(array, level, row)
                cor_ref[at : at + HALF_LON, :] = ref[level, KEEP_R + row, KEEP_C:COLS, :]
            for row in range(KEEP_R):
                at = lon_row(array, level, row)
                lon_ref[at : at + HALF_LON, :] = ref[level, row, KEEP_C:COLS, :]
    grad_up = tn(normed_ref[...], cot_up)
    grad_down = tn(cot, hidden)
    for k, grad in enumerate((grad_up, grad_down)):
        tiles = [grad[:, t * LANES : (t + 1) * LANES] for t in range(6)]
        halves = [jnp.concatenate(tiles[3 * h : 3 * h + 3], 0).reshape(8, CELLS, LANES) for h in range(2)]
        two_halves(*halves, keep_ref, send_ref, (slice(None), slice(k * CELLS, (k + 1) * CELLS), slice(None)))


def window_of(band, level, sector):
    return (band * LEV + level) * SECTORS + sector


def pieces(band, sector):
    for row in range(WIN_LAT):
        rolled = band * WIN_LAT + row
        edge = rolled < HALF_LAT
        line = rolled if edge else rolled - HALF_LAT
        if sector == 0:
            yield row, 0, HALF_LON, "cor" if edge else "lon", line, 0
            yield row, HALF_LON, HALF_LON, "lat" if edge else "own", line, 0
        else:
            yield row, 0, WIN_LON, "lat" if edge else "own", line, HALF_LON


def strip_row(source, array, level, line, column):
    place = {"lat": lat_row, "lon": lon_row, "cor": cor_row}[source]
    return place(array, level, line) + column


def attention_kernel(
    in_second_ref, grad_first_ref, lat_ref, lon_ref, cor_ref,
    bias_ref, gain_ref, qkv_ref, proj_ref, gain_mlp_ref,
    own_f_ref, own_c_ref, out_lat_ref, out_lon_ref, out_cor_ref, bias_out_ref, keep_ref, send_ref,
    x_ref, g_ref, q_ref, k_ref, v_ref, ca_ref, att_ref, cq_ref, ck_ref, cv_ref,
):
    strips = {"lat": lat_ref, "lon": lon_ref, "cor": cor_ref}
    for band in range(BANDS):
        for level in range(LEV):
            initial = (level - LEV // 2) % LEV
            for sector in range(SECTORS):
                base = window_of(band, level, sector) * CELLS
                for row, col, count, source, line, start in pieces(band, sector):
                    at = base + row * WIN_LON + col
                    for array, (dst, own) in enumerate(((x_ref, in_second_ref), (g_ref, grad_first_ref))):
                        if source == "own":
                            dst[at : at + count, :] = own[initial, line, start : start + count, :]
                        else:
                            src = strip_row(source, array, initial, line, start)
                            dst[at : at + count, :] = strips[source][src : src + count, :]
    gain = gain_ref[...]
    unit_field, inverse = norm_parts(x_ref[...])
    normed = (unit_field * gain).astype(bf16)
    weights_qkv = [qkv_ref[:, i * D : (i + 1) * D] for i in range(3)]
    w_proj = proj_ref[...]
    for ref, weight in zip((q_ref, k_ref, v_ref), weights_qkv):
        ref[...] = nn(normed, weight).astype(bf16).astype(f32)
    cot_low = g_ref[...].astype(bf16)
    ca_ref[...] = nt(cot_low, w_proj).astype(bf16).astype(f32)

    lane_head = lax.broadcasted_iota(jnp.int32, (CELLS, D), 1) // HEAD_DIM
    of_head = [lane_head == h for h in range(HEADS)]
    pad = jnp.zeros((LANES - CELLS, D), f32)

    def stacked(value):
        return jnp.concatenate([jnp.where(m, value, 0.0) for m in of_head], 0).astype(bf16)

    def gathered(value):
        total = jnp.where(of_head[0], value[:CELLS], 0.0)
        for h in range(1, HEADS):
            total = jnp.where(of_head[h], value[h * CELLS : (h + 1) * CELLS], total)
        return total

    first_band = lax.axis_index("lat") == 0
    query_low = lax.broadcasted_iota(jnp.int32, (CELLS, LANES), 0) < CELLS // 2
    key = lax.broadcasted_iota(jnp.int32, (CELLS, LANES), 1)
    apart = jnp.logical_and(query_low != (key < CELLS // 2), first_band)
    lane = lax.broadcasted_iota(jnp.int32, (STACK, LANES), 1)
    bias_grads = []
    for band in range(BANDS):
        for level in range(LEV):
            tables = []
            low = level * CELLS
            for h in range(HEADS):
                table = bias_ref[band, 0, h].astype(f32)[low : low + CELLS, low : low + CELLS]
                table = jnp.concatenate([table, jnp.full((CELLS, LANES - CELLS), padded_score, f32)], 1)
                if band == 0:
                    table = jnp.where(jnp.logical_and(apart, key < CELLS), masked_score, table)
                tables.append(table)
            table = jnp.concatenate(tables, 0)
            bias_grad = None
            for sector in range(SECTORS):
                base = window_of(band, level, sector) * CELLS
                part = slice(base, base + CELLS)
                queries = stacked(q_ref[part, :])
                key_part = jnp.concatenate([k_ref[part, :], pad], 0).astype(bf16)
                value_part = jnp.concatenate([v_ref[part, :], pad], 0).astype(bf16)
                scores = nt(queries, key_part) * score_scale + table
                exponent = jnp.exp(scores - jnp.max(scores, -1, keepdims=True))
                probability = exponent * (1.0 / jnp.sum(exponent, -1, keepdims=True))
                weights = probability.astype(bf16)
                att_ref[part, :] = gathered(nn(weights, value_part))
                cot_att = stacked(ca_ref[part, :])
                cot_weights = nt(cot_att, value_part)
                cv_ref[part, :] = tn(weights, cot_att)[:CELLS]
                inner = jnp.sum(cot_weights * probability, -1, keepdims=True)
                cot_scores = probability * (cot_weights - inner)
                bias_grad = cot_scores if bias_grad is None else bias_grad + cot_scores
                scaled = (cot_scores * score_scale).astype(bf16)
                cq_ref[part, :] = gathered(nn(scaled, key_part))
                ck_ref[part, :] = tn(scaled, queries)[:CELLS]
            bias_grads.append(bias_grad)
    left = [
        jnp.where(lane < 64, bias_grads[2 * b], pltpu.roll(bias_grads[2 * b + 1], 64, 1))
        for b in range(BANDS)
    ]
    lane3 = lane[: STACK // 3]
    rest = jnp.zeros((STACK // 3, LANES), f32)
    for g in range(3):
        for k in range(4):
            place = g * 32 + k * 8
            piece = bias_grads[k][g * (STACK // 3) : (g + 1) * (STACK // 3)]
            inside = jnp.logical_and(lane3 >= place, lane3 < place + 8)
            rest = jnp.where(inside, pltpu.roll(piece, (place - 64) % LANES, 1), rest)
    packed = jnp.concatenate([*left, rest, jnp.zeros((16, LANES), f32)], 0)
    bias_out_ref[...] = packed.reshape(16, 64, LANES)

    attended = att_ref[...].astype(bf16)
    branch = nn(attended, w_proj)
    grads = []
    cot_normed = None
    for ref, weight in zip((cq_ref, ck_ref, cv_ref), weights_qkv):
        cot_part = ref[...].astype(bf16)
        grads.append(tn(normed, cot_part))
        term = nt(cot_part, weight)
        cot_normed = term if cot_normed is None else cot_normed + term
    grads.append(tn(attended, cot_low))
    gain_part = jnp.sum(cot_normed * unit_field, 0, keepdims=True)
    x_ref[...] = branch
    g_ref[...] = norm_back(cot_normed, gain, unit_field, inverse)
    out_strips = {"lat": out_lat_ref, "lon": out_lon_ref, "cor": out_cor_ref}
    for band in range(BANDS):
        for level in range(LEV):
            initial = (level - LEV // 2) % LEV
            for sector in range(SECTORS):
                base = window_of(band, level, sector) * CELLS
                for row, col, count, source, line, start in pieces(band, sector):
                    at = base + row * WIN_LON + col
                    for array, (src, own) in enumerate(((x_ref, own_f_ref), (g_ref, own_c_ref))):
                        if source == "own":
                            own[initial, line, start : start + count, :] = src[at : at + count, :]
                        else:
                            dst = strip_row(source, array, initial, line, start)
                            out_strips[source][dst : dst + count, :] = src[at : at + count, :]
    tiles = [g[:, :LANES] for g in grads]
    tiles += [jnp.concatenate([grads[i][:, LANES:], grads[i + 1][:, LANES:]], 1) for i in (0, 2)]
    halves = [jnp.concatenate(tiles[3 * h : 3 * h + 3], 0).reshape(8, CELLS, LANES) for h in range(2)]
    two_halves(*halves, keep_ref, send_ref, (slice(None), slice(0, CELLS), slice(None)))
    gains = jnp.concatenate([gain_mlp_ref[...], gain_part], 0)
    right = jnp.concatenate([gains[:, LANES:], jnp.zeros((2, LANES - 64), f32)], 1)
    block = jnp.concatenate([gains[:, :LANES], right, jnp.zeros((4, LANES), f32)], 0)
    for ref in (keep_ref, send_ref):
        ref[:, CELLS : CELLS + 8, :] = jnp.broadcast_to(block[None], (8, 8, LANES))


def join_kernel(bias_ref, attn_ref, ff_ref, out_ref):
    attn = jnp.sum(attn_ref[...], 0)
    weights = jnp.concatenate(
        [attn[:CELLS], jnp.sum(ff_ref[...], 0), attn[CELLS:], jnp.zeros((32, LANES), f32)], 0
    )
    out_ref[:, :64, :] = bias_ref[...]
    out_ref[:, 64:, :] = weights.reshape(16, 16, LANES)


def total_kernel(in_ref, out_ref):
    out_ref[...] = jnp.broadcast_to(jnp.sum(in_ref[...], 0)[None], out_ref.shape)


def spread_kernel(in_ref, out_ref):
    weights = in_ref[:, 64:, :].reshape(256, LANES)[: 3 * CELLS]
    out_ref[...] = jnp.broadcast_to(weights[None], out_ref.shape)


def last_kernel(
    sums_ref, mine_ref, other_ref,
    gain_attn_ref, qkv_ref, proj_ref, bias_ref, gain_mlp_ref, up_ref, down_ref,
):
    packed = sums_ref[:, :64, :].reshape(1024, LANES)
    lane = lax.broadcasted_iota(jnp.int32, (STACK, LANES), 1)
    third = STACK // 3
    rest = packed[2 * STACK : 2 * STACK + third]
    zeros = jnp.zeros((CELLS, LANES), f32)
    for band in range(BANDS):
        for level in range(LEV):
            table = packed[band * STACK : (band + 1) * STACK]
            if level == 1:
                table = pltpu.roll(table, 64, 1)
            k = band * LEV + level
            tail = jnp.concatenate([pltpu.roll(rest, (64 - g * 32 - k * 8) % LANES, 1) for g in range(3)], 0)
            table = jnp.where(lane < 64, table, jnp.where(lane < CELLS, tail, 0.0))
            for h in range(HEADS):
                rows = jnp.concatenate([table[h * CELLS : (h + 1) * CELLS], zeros], 1)
                if level == 1:
                    rows = pltpu.roll(rows, CELLS, 1)
                bias_ref[band, 0, h, level * CELLS : (level + 1) * CELLS, :] = rows[:, : 2 * CELLS]
    gains = sums_ref[:, 64:, :].reshape(256, LANES)[3 * CELLS : 3 * CELLS + 8]
    gains = jnp.concatenate([gains[:2], gains[2:4, :64]], 1)
    gain_mlp_ref[...] = gains[0:1]
    gain_attn_ref[...] = gains[1:2]
    own = lax.rem(lax.axis_index("lat"), 2) == 0
    mine, other = mine_ref[...], other_ref[...]
    halves = [jnp.where(own, mine, other), jnp.where(own, other, mine)]

    def tiles_of(k):
        found = []
        for half in halves:
            rows = half[:, k * CELLS : (k + 1) * CELLS].reshape(8 * CELLS, LANES)
            found += [rows[t * D : (t + 1) * D] for t in range(3)]
        return found

    tiles = tiles_of(0)
    parts = [
        jnp.concatenate([tiles[i], tiles[4 + i // 2][:, 64 * (i % 2) : 64 * (i % 2) + 64]], 1)
        for i in range(4)
    ]
    qkv_ref[...] = jnp.concatenate(parts[:3], 1)
    proj_ref[...] = parts[3]
    up_ref[...] = jnp.concatenate(tiles_of(1), 1)
    for t, tile in enumerate(tiles_of(2)):
        down_ref[t * LANES : (t + 1) * LANES, :] = tile.T


def stream_kernel(
    first_ref, cot_second_ref, own_f_ref, own_c_ref, lat_ref, lon_ref, cor_ref,
    in_first_ref, grad_second_ref, cot_ref,
):
    cot_ref[...] = cot_second_ref[...].astype(f32)
    inner = (slice(None), slice(0, KEEP_R), slice(0, KEEP_C))
    in_first_ref[inner] = first_ref[inner] - own_f_ref[inner]
    grad_second_ref[inner] = cot_ref[inner] + own_c_ref[inner]

    def edge(level, row, cols, ref, place):
        count = cols.stop - cols.start
        at = place(0)
        in_first_ref[level, row, cols] = first_ref[level, row, cols] - ref[at : at + count, :]
        at = place(1)
        grad_second_ref[level, row, cols] = cot_ref[level, row, cols] + ref[at : at + count, :]

    for level in range(LEV):
        for row in range(HALF_LAT):
            edge(level, KEEP_R + row, slice(0, KEEP_C), lat_ref, lambda a: lat_row(a, level, row))
            edge(level, KEEP_R + row, slice(KEEP_C, COLS), cor_ref, lambda a: cor_row(a, level, row))
        for row in range(KEEP_R):
            edge(level, row, slice(KEEP_C, COLS), lon_ref, lambda a: lon_row(a, level, row))


def kernel(fn, out_shape, scratch=(), name=None, flops=0, nbytes=0):
    return pl.pallas_call(
        fn,
        out_shape=[jax.ShapeDtypeStruct(s, f32) for s in out_shape],
        scratch_shapes=[pltpu.VMEM(s, d) for s, d in scratch],
        compiler_params=pltpu.CompilerParams(vmem_limit_bytes=48 * 1024 * 1024),
        cost_estimate=pl.CostEstimate(flops=flops, bytes_accessed=nbytes, transcendentals=0),
        name=name,
    )


def body(
    out_first, out_second, cot_first, cot_second,
    gain_attn, w_qkv, w_proj, earth_bias, gain_mlp, w_up, w_down,
):
    lat_count, lon_count = lax.axis_size("lat"), lax.axis_size("lon")
    both = ("lat", "lon")
    shape = (LEV, ROWS, COLS, D)

    def halo(lat, lon, cor, by):
        ring = lambda n: [(i, (i + by) % n) for i in range(n)]
        diagonal = [
            (a * lon_count + o, ((a + by) % lat_count) * lon_count + (o + by) % lon_count)
            for a in range(lat_count)
            for o in range(lon_count)
        ]
        return (
            lax.ppermute(lat, "lat", ring(lat_count)),
            lax.ppermute(lon, "lon", ring(lon_count)),
            lax.ppermute(cor, both, diagonal),
        )

    def other_core(value):
        return lax.ppermute(value, "lat", [(i, i ^ 1) for i in range(lat_count)])

    same_core = [list(range(c, lat_count, 2)) for c in range(2)]

    def swap_lat(value):
        return lax.all_to_all(value, "lat", 0, 0, tiled=True, axis_index_groups=same_core)

    def swap_lon(value):
        return lax.all_to_all(value, "lon", 0, 0, tiled=True)

    strip_shapes = [(LAT_ROWS, D), (LON_ROWS, D), (COR_ROWS, D)]
    in_second, grad_first, lat, lon, cor, ff_keep, ff_send, gain_mlp_part = kernel(
        ff_kernel,
        [shape, shape, *strip_shapes, (8, 2 * CELLS, LANES), (8, 2 * CELLS, LANES), (1, D)],
        [((TOKENS, FF), bf16), ((TOKENS, FF), bf16), ((TOKENS, D), bf16)],
        "feedforward",
        flops=12 * TOKENS * D * FF,
        nbytes=6_000_000,
    )(out_first, out_second, cot_first, cot_second, gain_mlp.reshape(1, D), w_up, w_down)
    lat, lon, cor = halo(lat, lon, cor, 1)
    ff_parts = swap_lat(ff_keep + other_core(ff_send))
    own_f, own_c, lat, lon, cor, bias_part, at_keep, at_send = kernel(
        attention_kernel,
        [shape, shape, *strip_shapes, (16, 64, LANES), (8, CELLS + 8, LANES), (8, CELLS + 8, LANES)],
        [((TOKENS, D), f32)] * 10,
        "attention",
        flops=4_000_000_000,
        nbytes=6_000_000,
    )(
        in_second, grad_first, lat, lon, cor,
        earth_bias, gain_attn.reshape(1, D), w_qkv, w_proj, gain_mlp_part,
    )
    lat, lon, cor = halo(lat, lon, cor, -1)
    at_parts = swap_lat(at_keep + other_core(at_send))
    (joined,) = kernel(join_kernel, [(16, 80, LANES)], name="join")(bias_part, at_parts, ff_parts)
    (totals,) = kernel(total_kernel, [(16, 80, LANES)], name="total")(swap_lon(joined))
    sums = swap_lon(totals)
    (spread,) = kernel(spread_kernel, [(8, 3 * CELLS, LANES)], name="spread")(sums)
    mine = swap_lat(spread)
    other = other_core(mine)
    in_first, grad_second = kernel(
        stream_kernel, [shape, shape], [(shape, f32)], "streams", nbytes=3_000_000
    )(out_first, cot_second, own_f, own_c, lat, lon, cor)
    grad_gain_attn, grad_qkv, grad_proj, grad_bias, grad_gain_mlp, grad_up, grad_down = kernel(
        last_kernel,
        [(1, D), (D, 3 * D), (D, D), (BANDS, 1, HEADS, 2 * CELLS, 2 * CELLS), (1, D), (D, FF), (FF, D)],
        name="last",
        nbytes=6_000_000,
    )(sums, mine, other)
    return (
        in_first, in_second, grad_first, grad_second,
        grad_gain_attn.reshape(D), grad_qkv, grad_proj, grad_bias,
        grad_gain_mlp.reshape(D), grad_up, grad_down,
    )


def solution(mesh):
    field = P(None, "lat", "lon", None)
    placed = (field,) * 4 + (P(), P(), P(), P("lat", None, None, None, None), P(), P(), P())
    return jax.shard_map(body, mesh=mesh, in_specs=placed, out_specs=placed, check_vma=False)
```

```python
import jax
import jax.numpy as jnp
from jax import lax
from jax.experimental import pallas as pl
from jax.experimental.pallas import tpu as pltpu
from jax.sharding import PartitionSpec as P

HEADS = 6
HEAD_DIM = 32
D = 192
FF = 768
LEV = 2
WIN_LAT = 6
WIN_LON = 12
CELLS = WIN_LAT * WIN_LON
BANDS = 2
SECTORS = 2
ROWS = BANDS * WIN_LAT
COLS = SECTORS * WIN_LON
TOKENS = LEV * ROWS * COLS
HALF_LAT = WIN_LAT // 2
HALF_LON = WIN_LON // 2
STACK = HEADS * CELLS
LANES = 128

norm_eps = 1e-05
gelu_scale = 0.7978845608028654
gelu_cubic = 0.044715
masked_score = -1000000000.0
padded_score = -1e30
score_scale = HEAD_DIM ** (-0.5)

f32 = jnp.float32
bf16 = jnp.bfloat16


def nn(a, b):
    return lax.dot_general(a, b, (((1,), (0,)), ((), ())), preferred_element_type=f32)


def nt(a, b):
    return lax.dot_general(a, b, (((1,), (1,)), ((), ())), preferred_element_type=f32)


def tn(a, b):
    return lax.dot_general(a, b, (((0,), (0,)), ((), ())), preferred_element_type=f32)


def norm_parts(field):
    average = jnp.mean(field, -1, keepdims=True)
    centred = field - average
    inverse = lax.rsqrt(jnp.mean(centred * centred, -1, keepdims=True) + norm_eps)
    return (centred * inverse, inverse)


def norm_back(cot_normed, norm_gain, unit_field, inverse):
    cot_unit = cot_normed * norm_gain
    return inverse * (
        cot_unit
        - jnp.mean(cot_unit, -1, keepdims=True)
        - unit_field * jnp.mean(cot_unit * unit_field, -1, keepdims=True)
    )


def two_halves(first, second, keep_ref, send_ref, where):
    mine = lax.rem(lax.axis_index("lat"), 2) == 0
    keep_ref[where] = jnp.where(mine, first, second)
    send_ref[where] = jnp.where(mine, second, first)


def lat_row(array, level, row):
    return ((array * LEV + level) * HALF_LAT + row) * (COLS - HALF_LON)


def lon_row(array, level, row):
    return ((array * LEV + level) * (ROWS - HALF_LAT) + row) * HALF_LON


def cor_row(array, level, row):
    return ((array * LEV + level) * HALF_LAT + row) * HALF_LON


LAT_ROWS = lat_row(2, 0, 0)
LON_ROWS = lon_row(2, 0, 0)
COR_ROWS = cor_row(2, 0, 0)
KEEP_R = ROWS - HALF_LAT
KEEP_C = COLS - HALF_LON


def ff_kernel(
    first_hbm, second_hbm, cot_first_hbm, cot_second_hbm, gain_ref, up_hbm, down_hbm,
    in_second_hbm, grad_first_hbm, x_ref, g_ref, lat_ref, lon_ref, cor_ref, keep_ref, send_ref, gain_out_ref,
    first_ref, second_ref, cot_first_ref, cot_second_ref, up_ref, down_ref,
    in_second_ref, grad_first_ref, hidden_ref, cot_up_ref, normed_ref, in_sems, out_sems,
):
    sources = (first_hbm, up_hbm, cot_second_hbm, down_hbm, second_hbm, cot_first_hbm)
    targets = (first_ref, up_ref, cot_second_ref, down_ref, second_ref, cot_first_ref)
    loads = [pltpu.make_async_copy(x, y, in_sems.at[i]) for i, (x, y) in enumerate(zip(sources, targets))]
    for load in loads:
        load.start()
    loads[0].wait()
    tokens = first_ref[...].reshape(TOKENS, D)
    gain = gain_ref[...]
    unit_field, inverse = norm_parts(tokens)
    normed_ref[...] = (unit_field * gain).astype(bf16)
    for load in loads[1:4]:
        load.wait()
    cot = cot_second_ref[...].astype(f32).reshape(TOKENS, D).astype(bf16)
    w_up = up_ref[...]
    w_down_t = down_ref[...]
    step = 96
    for i in range(TOKENS // step):
        part = pl.ds(i * step, step)
        up_proj = nn(normed_ref[part, :], w_up)
        square = up_proj * up_proj
        half = 0.5 * (1.0 + jnp.tanh(up_proj * (gelu_scale + gelu_scale * gelu_cubic * square)))
        hidden_ref[part, :] = (up_proj * half).astype(bf16)
        cot_hidden = nn(cot[i * step : (i + 1) * step], w_down_t)
        slope = half + (half * (1.0 - half)) * up_proj * (
            2.0 * gelu_scale + 6.0 * gelu_scale * gelu_cubic * square
        )
        cot_up_ref[part, :] = (cot_hidden * slope).astype(bf16)
    hidden = hidden_ref[...]
    cot_up = cot_up_ref[...]
    shape = (LEV, ROWS, COLS, D)
    loads[4].wait()
    in_second_ref[...] = second_ref[...] - nt(hidden, w_down_t).reshape(shape)
    stores = [
        pltpu.make_async_copy(in_second_ref, in_second_hbm, out_sems.at[0]),
        pltpu.make_async_copy(grad_first_ref, grad_first_hbm, out_sems.at[1]),
    ]
    stores[0].start()
    cot_normed = nt(cot_up, w_up)
    gain_out_ref[...] = jnp.sum(cot_normed * unit_field, 0, keepdims=True)
    back = norm_back(cot_normed, gain, unit_field, inverse)
    loads[5].wait()
    grad_first_ref[...] = cot_first_ref[...].astype(f32) + back.reshape(shape)
    stores[1].start()
    for array, ref in enumerate((in_second_ref, grad_first_ref)):
        for level in range(LEV):
            for row in range(HALF_LAT):
                at = lat_row(array, level, row)
                lat_ref[at : at + KEEP_C, :] = ref[level, KEEP_R + row, 0:KEEP_C, :]
                at = cor_row(array, level, row)
                cor_ref[at : at + HALF_LON, :] = ref[level, KEEP_R + row, KEEP_C:COLS, :]
            for row in range(KEEP_R):
                at = lon_row(array, level, row)
                lon_ref[at : at + HALF_LON, :] = ref[level, row, KEEP_C:COLS, :]
    for at, count, source, level, line, start in all_pieces():
        if source == "own":
            x_ref[at : at + count, :] = in_second_ref[level, line, start : start + count, :]
            g_ref[at : at + count, :] = grad_first_ref[level, line, start : start + count, :]
    grad_up = tn(normed_ref[...], cot_up)
    grad_down = tn(cot, hidden)
    for k, grad in enumerate((grad_up, grad_down)):
        tiles = [grad[:, t * LANES : (t + 1) * LANES] for t in range(6)]
        halves = [jnp.concatenate(tiles[3 * h : 3 * h + 3], 0).reshape(8, CELLS, LANES) for h in range(2)]
        two_halves(*halves, keep_ref, send_ref, (slice(None), slice(k * CELLS, (k + 1) * CELLS), slice(None)))
    for store in stores:
        store.wait()


def window_of(band, level, sector):
    return (band * LEV + level) * SECTORS + sector


def pieces(band, sector):
    for row in range(WIN_LAT):
        rolled = band * WIN_LAT + row
        edge = rolled < HALF_LAT
        line = rolled if edge else rolled - HALF_LAT
        if sector == 0:
            yield row, 0, HALF_LON, "cor" if edge else "lon", line, 0
            yield row, HALF_LON, HALF_LON, "lat" if edge else "own", line, 0
        else:
            yield row, 0, WIN_LON, "lat" if edge else "own", line, HALF_LON


def strip_row(source, array, level, line, column):
    place = {"lat": lat_row, "lon": lon_row, "cor": cor_row}[source]
    return place(array, level, line) + column


def all_pieces():
    for band in range(BANDS):
        for level in range(LEV):
            initial = (level - LEV // 2) % LEV
            for sector in range(SECTORS):
                base = window_of(band, level, sector) * CELLS
                for row, col, count, source, line, start in pieces(band, sector):
                    yield base + row * WIN_LON + col, count, source, initial, line, start


def attention_kernel(
    x_in_ref, g_in_ref, lat_ref, lon_ref, cor_ref,
    bias_ref, gain_ref, qkv_ref, proj_ref, gain_mlp_ref,
    win_f_ref, win_c_ref, out_lat_ref, out_lon_ref, out_cor_ref, bias_out_ref, keep_ref, send_ref,
    x_ref, g_ref, q_ref, k_ref, v_ref, ca_ref, att_ref, cq_ref, ck_ref, cv_ref,
):
    strips = {"lat": lat_ref, "lon": lon_ref, "cor": cor_ref}
    for at, count, source, level, line, start in all_pieces():
        for array, (dst, own) in enumerate(((x_ref, x_in_ref), (g_ref, g_in_ref))):
            if source == "own":
                dst[at : at + count, :] = own[at : at + count, :]
            else:
                src = strip_row(source, array, level, line, start)
                dst[at : at + count, :] = strips[source][src : src + count, :]
    gain = gain_ref[...]
    unit_field, inverse = norm_parts(x_ref[...])
    normed = (unit_field * gain).astype(bf16)
    weights_qkv = [qkv_ref[:, i * D : (i + 1) * D] for i in range(3)]
    w_proj = proj_ref[...]
    for ref, weight in zip((q_ref, k_ref, v_ref), weights_qkv):
        ref[...] = nn(normed, weight).astype(bf16).astype(f32)
    cot_low = g_ref[...].astype(bf16)
    ca_ref[...] = nt(cot_low, w_proj).astype(bf16).astype(f32)

    lane_head = lax.broadcasted_iota(jnp.int32, (CELLS, D), 1) // HEAD_DIM
    of_head = [lane_head == h for h in range(HEADS)]
    pad = jnp.zeros((LANES - CELLS, D), f32)

    def stacked(value):
        return jnp.concatenate([jnp.where(m, value, 0.0) for m in of_head], 0).astype(bf16)

    def gathered(value):
        total = jnp.where(of_head[0], value[:CELLS], 0.0)
        for h in range(1, HEADS):
            total = jnp.where(of_head[h], value[h * CELLS : (h + 1) * CELLS], total)
        return total

    first_band = lax.axis_index("lat") == 0
    query_low = lax.broadcasted_iota(jnp.int32, (CELLS, LANES), 0) < CELLS // 2
    key = lax.broadcasted_iota(jnp.int32, (CELLS, LANES), 1)
    apart = jnp.logical_and(query_low != (key < CELLS // 2), first_band)
    lane = lax.broadcasted_iota(jnp.int32, (STACK, LANES), 1)
    bias_grads = []
    for band in range(BANDS):
        for level in range(LEV):
            tables = []
            low = level * CELLS
            for h in range(HEADS):
                table = bias_ref[band, 0, h].astype(f32)[low : low + CELLS, low : low + CELLS]
                table = jnp.concatenate([table, jnp.full((CELLS, LANES - CELLS), padded_score, f32)], 1)
                if band == 0:
                    table = jnp.where(jnp.logical_and(apart, key < CELLS), masked_score, table)
                tables.append(table)
            table = jnp.concatenate(tables, 0)
            bias_grad = None
            for sector in range(SECTORS):
                base = window_of(band, level, sector) * CELLS
                part = slice(base, base + CELLS)
                queries = stacked(q_ref[part, :])
                key_part = jnp.concatenate([k_ref[part, :], pad], 0).astype(bf16)
                value_part = jnp.concatenate([v_ref[part, :], pad], 0).astype(bf16)
                scores = nt(queries, key_part) * score_scale + table
                exponent = jnp.exp(scores - jnp.max(scores, -1, keepdims=True))
                probability = exponent * (1.0 / jnp.sum(exponent, -1, keepdims=True))
                weights = probability.astype(bf16)
                att_ref[part, :] = gathered(nn(weights, value_part))
                cot_att = stacked(ca_ref[part, :])
                cot_weights = nt(cot_att, value_part)
                cv_ref[part, :] = tn(weights, cot_att)[:CELLS]
                inner = jnp.sum(cot_weights * probability, -1, keepdims=True)
                cot_scores = probability * (cot_weights - inner)
                bias_grad = cot_scores if bias_grad is None else bias_grad + cot_scores
                scaled = (cot_scores * score_scale).astype(bf16)
                cq_ref[part, :] = gathered(nn(scaled, key_part))
                ck_ref[part, :] = tn(scaled, queries)[:CELLS]
            bias_grads.append(bias_grad)
    left = [
        jnp.where(lane < 64, bias_grads[2 * b], pltpu.roll(bias_grads[2 * b + 1], 64, 1))
        for b in range(BANDS)
    ]
    lane3 = lane[: STACK // 3]
    rest = jnp.zeros((STACK // 3, LANES), f32)
    for g in range(3):
        for k in range(4):
            place = g * 32 + k * 8
            piece = bias_grads[k][g * (STACK // 3) : (g + 1) * (STACK // 3)]
            inside = jnp.logical_and(lane3 >= place, lane3 < place + 8)
            rest = jnp.where(inside, pltpu.roll(piece, (place - 64) % LANES, 1), rest)
    packed = jnp.concatenate([*left, rest, jnp.zeros((16, LANES), f32)], 0)
    bias_out_ref[...] = packed.reshape(16, 64, LANES)

    attended = att_ref[...].astype(bf16)
    branch = nn(attended, w_proj)
    grads = []
    cot_normed = None
    for ref, weight in zip((cq_ref, ck_ref, cv_ref), weights_qkv):
        cot_part = ref[...].astype(bf16)
        grads.append(tn(normed, cot_part))
        term = nt(cot_part, weight)
        cot_normed = term if cot_normed is None else cot_normed + term
    grads.append(tn(attended, cot_low))
    gain_part = jnp.sum(cot_normed * unit_field, 0, keepdims=True)
    win_f_ref[...] = branch
    win_c_ref[...] = norm_back(cot_normed, gain, unit_field, inverse)
    out_strips = {"lat": out_lat_ref, "lon": out_lon_ref, "cor": out_cor_ref}
    for at, count, source, level, line, start in all_pieces():
        if source != "own":
            for array, src in enumerate((win_f_ref, win_c_ref)):
                dst = strip_row(source, array, level, line, start)
                out_strips[source][dst : dst + count, :] = src[at : at + count, :]
    tiles = [g[:, :LANES] for g in grads]
    tiles += [jnp.concatenate([grads[i][:, LANES:], grads[i + 1][:, LANES:]], 1) for i in (0, 2)]
    halves = [jnp.concatenate(tiles[3 * h : 3 * h + 3], 0).reshape(8, CELLS, LANES) for h in range(2)]
    two_halves(*halves, keep_ref, send_ref, (slice(None), slice(0, CELLS), slice(None)))
    gains = jnp.concatenate([gain_mlp_ref[...], gain_part], 0)
    right = jnp.concatenate([gains[:, LANES:], jnp.zeros((2, LANES - 64), f32)], 1)
    block = jnp.concatenate([gains[:, :LANES], right, jnp.zeros((4, LANES), f32)], 0)
    for ref in (keep_ref, send_ref):
        ref[:, CELLS:, :] = jnp.broadcast_to(block[None], (8, 8, LANES))


def add_kernel(a_ref, b_ref, out_ref):
    out_ref[...] = a_ref[...] + b_ref[...]


def lat_bit(k):
    return lax.rem(lax.axis_index("lat") // (1 << k), 2)


def lat_join_kernel(keep_ref, recv_ref, ff_ref, out_ref):
    out_ref[:, : CELLS + 8, :] = keep_ref[...] + recv_ref[...]
    out_ref[:, CELLS + 8 :, :] = ff_ref[...]


def lon_join_kernel(bias_ref, parts_ref, out_ref):
    total = jnp.sum(parts_ref[...], 0)
    weights = jnp.concatenate(
        [total[:CELLS], total[CELLS + 8 :], total[CELLS : CELLS + 8], jnp.zeros((32, LANES), f32)], 0
    )
    out_ref[:, :64, :] = bias_ref[...]
    out_ref[:, 64:, :] = weights.reshape(16, 16, LANES)


def total_kernel(in_ref, out_ref):
    out_ref[...] = jnp.broadcast_to(jnp.sum(in_ref[...], 0)[None], out_ref.shape)


def spread_kernel(in_ref, out_ref, gains_ref):
    weights = in_ref[:, 64:, :].reshape(256, LANES)
    out_ref[...] = jnp.broadcast_to(weights[None, : 3 * CELLS], out_ref.shape)
    gains_ref[...] = weights[3 * CELLS : 3 * CELLS + 8]


def bias_kernel(sums_ref, bias_ref):
    packed = sums_ref[:, :64, :].reshape(1024, LANES)
    lane = lax.broadcasted_iota(jnp.int32, (STACK, LANES), 1)
    third = STACK // 3
    rest = packed[2 * STACK : 2 * STACK + third]
    zeros = jnp.zeros((CELLS, LANES), f32)
    for band in range(BANDS):
        for level in range(LEV):
            table = packed[band * STACK : (band + 1) * STACK]
            if level == 1:
                table = pltpu.roll(table, 64, 1)
            k = band * LEV + level
            tail = jnp.concatenate([pltpu.roll(rest, (64 - g * 32 - k * 8) % LANES, 1) for g in range(3)], 0)
            table = jnp.where(lane < 64, table, jnp.where(lane < CELLS, tail, 0.0))
            for h in range(HEADS):
                rows = jnp.concatenate([table[h * CELLS : (h + 1) * CELLS], zeros], 1)
                if level == 1:
                    rows = pltpu.roll(rows, CELLS, 1)
                bias_ref[band, 0, h, level * CELLS : (level + 1) * CELLS, :] = rows[:, : 2 * CELLS]


def last_kernel(
    gains_in_ref, mine_ref, other_ref,
    gain_attn_ref, qkv_ref, proj_ref, gain_mlp_ref, up_ref, down_ref,
):
    gains = gains_in_ref[...]
    gains = jnp.concatenate([gains[:2], gains[2:4, :64]], 1)
    gain_mlp_ref[...] = gains[0:1]
    gain_attn_ref[...] = gains[1:2]
    own = lat_bit(0) == 0
    mine, other = mine_ref[...], other_ref[...]
    halves = [jnp.where(own, mine, other), jnp.where(own, other, mine)]

    def tiles_of(k):
        found = []
        for half in halves:
            rows = half[:, k * CELLS : (k + 1) * CELLS].reshape(8 * CELLS, LANES)
            found += [rows[t * D : (t + 1) * D] for t in range(3)]
        return found

    tiles = tiles_of(0)
    parts = [
        jnp.concatenate([tiles[i], tiles[4 + i // 2][:, 64 * (i % 2) : 64 * (i % 2) + 64]], 1)
        for i in range(4)
    ]
    qkv_ref[...] = jnp.concatenate(parts[:3], 1)
    proj_ref[...] = parts[3]
    up_ref[...] = jnp.concatenate(tiles_of(1), 1)
    down_ref[...] = jnp.concatenate(tiles_of(2), 1)


def stream_kernel(
    first_ref, cot_second_ref, win_f_ref, win_c_ref, lat_ref, lon_ref, cor_ref,
    in_first_ref, grad_second_ref, cot_ref,
):
    cot_ref[...] = cot_second_ref[...].astype(f32)
    strips = {"lat": lat_ref, "lon": lon_ref, "cor": cor_ref}
    for at, count, source, level, line, start in all_pieces():
        if source == "own":
            f_part, c_part = (ref[at : at + count, :] for ref in (win_f_ref, win_c_ref))
            row, col = line, start
        else:
            row = line + (0 if source == "lon" else KEEP_R)
            col = start + (0 if source == "lat" else KEEP_C)
            at_f, at_c = (strip_row(source, array, level, line, start) for array in range(2))
            f_part, c_part = (strips[source][p : p + count, :] for p in (at_f, at_c))
        spot = (level, row, slice(col, col + count))
        in_first_ref[spot] = first_ref[spot] - f_part
        grad_second_ref[spot] = cot_ref[spot] + c_part


def kernel(fn, out_shape, scratch=(), name=None, flops=0, nbytes=0, in_hbm=(), out_hbm=()):
    def spec(far):
        return pl.BlockSpec(memory_space=pltpu.HBM if far else pltpu.VMEM)

    def in_specs(count):
        return [spec(i in in_hbm) for i in range(count)]

    def call(*args):
        args = [
            pltpu.with_memory_space_constraint(x, pltpu.HBM) if i in in_hbm else x
            for i, x in enumerate(args)
        ]
        return pl.pallas_call(
            fn,
            out_shape=[jax.ShapeDtypeStruct(s, f32) for s in out_shape],
            in_specs=in_specs(len(args)),
            out_specs=[spec(i in out_hbm) for i in range(len(out_shape))],
            scratch_shapes=[s if not isinstance(s, tuple) else pltpu.VMEM(*s) for s in scratch],
            compiler_params=pltpu.CompilerParams(vmem_limit_bytes=32 * 1024 * 1024),
            cost_estimate=pl.CostEstimate(flops=flops, bytes_accessed=nbytes, transcendentals=0),
            name=name,
        )(*args)

    return call


def body(
    out_first, out_second, cot_first, cot_second,
    gain_attn, w_qkv, w_proj, earth_bias, gain_mlp, w_up, w_down,
):
    lat_count, lon_count = lax.axis_size("lat"), lax.axis_size("lon")
    both = ("lat", "lon")
    shape = (LEV, ROWS, COLS, D)

    def halo(lat, lon, cor, by):
        ring = lambda n: [(i, (i + by) % n) for i in range(n)]
        diagonal = [
            (a * lon_count + o, ((a + by) % lat_count) * lon_count + (o + by) % lon_count)
            for a in range(lat_count)
            for o in range(lon_count)
        ]
        return (
            lax.ppermute(lat, "lat", ring(lat_count)),
            lax.ppermute(lon, "lon", ring(lon_count)),
            lax.ppermute(cor, both, diagonal),
        )

    same_core = [list(range(c, lat_count, 2)) for c in range(2)]

    def swap_lat(value):
        return lax.all_to_all(value, "lat", 0, 0, tiled=True, axis_index_groups=same_core)

    def swap_lon(value):
        return lax.all_to_all(value, "lon", 0, 0, tiled=True)

    def across(value, bit):
        return lax.ppermute(value, "lat", [(i, i ^ (1 << bit)) for i in range(lat_count)])

    strip_shapes = [(LAT_ROWS, D), (LON_ROWS, D), (COR_ROWS, D)]
    win = (TOKENS, D)
    ff_half = (8, 2 * CELLS, LANES)
    in_second, grad_first, x_win, g_win, lat, lon, cor, ff_keep, ff_send, gain_mlp_part = kernel(
        ff_kernel,
        [shape, shape, win, win, *strip_shapes, ff_half, ff_half, (1, D)],
        [
            (shape, f32), (shape, f32), (shape, bf16), (shape, bf16), ((D, FF), bf16), ((D, FF), bf16),
            (shape, f32), (shape, f32), ((TOKENS, FF), bf16), ((TOKENS, FF), bf16), ((TOKENS, D), bf16),
            pltpu.SemaphoreType.DMA((6,)), pltpu.SemaphoreType.DMA((2,)),
        ],
        "feedforward",
        flops=12 * TOKENS * D * FF,
        nbytes=6_000_000,
        in_hbm=(0, 1, 2, 3, 5, 6),
        out_hbm=(0, 1),
    )(out_first, out_second, cot_first, cot_second, gain_mlp.reshape(1, D), w_up, w_down.T)
    lat, lon, cor = halo(lat, lon, cor, 1)
    (ff_sum,) = kernel(add_kernel, [ff_half], name="pair")(ff_keep, across(ff_send, 0))
    x_win, ff_sum = lax.optimization_barrier((x_win, ff_sum))
    at_half = (8, CELLS + 8, LANES)
    win_f, win_c, lat, lon, cor, bias_part, keep, send = kernel(
        attention_kernel,
        [win, win, *strip_shapes, (16, 64, LANES), at_half, at_half],
        [(win, f32)] * 10,
        "attention",
        flops=16_000_000_000,
        nbytes=16_000_000,
    )(
        x_win, g_win, lat, lon, cor,
        earth_bias, gain_attn.reshape(1, D), w_qkv, w_proj, gain_mlp_part,
    )
    lat, lon, cor = halo(lat, lon, cor, -1)
    (parts,) = kernel(lat_join_kernel, [(8, 3 * CELLS + 8, LANES)], name="latjoin")(
        keep, across(send, 0), ff_sum
    )
    parts = swap_lat(parts)
    parts, lat, lon, cor = lax.optimization_barrier((parts, lat, lon, cor))
    (joined,) = kernel(lon_join_kernel, [(16, 80, LANES)], name="lonjoin")(bias_part, parts)
    (totals,) = kernel(total_kernel, [(16, 80, LANES)], name="total")(swap_lon(joined))
    sums = swap_lon(totals)
    spread, gains = kernel(spread_kernel, [(8, 3 * CELLS, LANES), (8, LANES)], name="spread")(sums)
    mine = swap_lat(spread)
    other = across(mine, 0)
    in_first, grad_second = kernel(
        stream_kernel, [shape, shape], [(shape, f32)], "streams", nbytes=3_000_000, flops=2_000_000_000
    )(out_first, cot_second, win_f, win_c, lat, lon, cor)
    (grad_bias,) = kernel(bias_kernel, [(BANDS, 1, HEADS, 2 * CELLS, 2 * CELLS)], name="bias")(sums)
    grad_gain_attn, grad_qkv, grad_proj, grad_gain_mlp, grad_up, grad_down = kernel(
        last_kernel,
        [(1, D), (D, 3 * D), (D, D), (1, D), (D, FF), (D, FF)],
        name="last",
        nbytes=6_000_000,
    )(gains, mine, other)
    return (
        in_first, in_second, grad_first, grad_second,
        grad_gain_attn.reshape(D), grad_qkv, grad_proj, grad_bias,
        grad_gain_mlp.reshape(D), grad_up, grad_down.T,
    )


def solution(mesh):
    field = P(None, "lat", "lon", None)
    placed = (field,) * 4 + (P(), P(), P(), P("lat", None, None, None, None), P(), P(), P())
    return jax.shard_map(body, mesh=mesh, in_specs=placed, out_specs=placed, check_vma=False)
```

```python
import functools

import jax
import jax.numpy as jnp
from jax import lax
from jax.experimental import pallas as pl
from jax.experimental.pallas import tpu as pltpu
from jax.sharding import PartitionSpec as P

HEADS = 6
HEAD_DIM = 32
D = 192
FF = 768
LEV = 2
WIN_LAT = 6
WIN_LON = 12
CELLS = WIN_LAT * WIN_LON
BANDS = 2
CHIPS = 16
PART = 3 * 192 // 16
SECTORS = 2
ROWS = BANDS * WIN_LAT
COLS = SECTORS * WIN_LON
TOKENS = LEV * ROWS * COLS
HALF_LAT = WIN_LAT // 2
HALF_LON = WIN_LON // 2
STACK = HEADS * CELLS
LANES = 128

norm_eps = 1e-05
gelu_scale = 0.7978845608028654
gelu_cubic = 0.044715
masked_score = -1000000000.0
padded_score = -1e30
score_scale = HEAD_DIM ** (-0.5)

f32 = jnp.float32
bf16 = jnp.bfloat16


def nn(a, b):
    return lax.dot_general(a, b, (((1,), (0,)), ((), ())), preferred_element_type=f32)


def nt(a, b):
    return lax.dot_general(a, b, (((1,), (1,)), ((), ())), preferred_element_type=f32)


def tn(a, b):
    return lax.dot_general(a, b, (((0,), (0,)), ((), ())), preferred_element_type=f32)


def norm_parts(field):
    average = jnp.mean(field, -1, keepdims=True)
    centred = field - average
    inverse = lax.rsqrt(jnp.mean(centred * centred, -1, keepdims=True) + norm_eps)
    return (centred * inverse, inverse)


def norm_back(cot_normed, norm_gain, unit_field, inverse):
    cot_unit = cot_normed * norm_gain
    return inverse * (
        cot_unit
        - jnp.mean(cot_unit, -1, keepdims=True)
        - unit_field * jnp.mean(cot_unit * unit_field, -1, keepdims=True)
    )


def half_at(by):
    x = lax.axis_index("lon") // 8 * 2 + lax.axis_index("lat") // 8
    return lax.rem(x + by, 4) // 2


def lat_bit(k):
    return lax.rem(lax.axis_index("lat") // (1 << k), 2)


def lat_row(array, level, row):
    return ((array * LEV + level) * HALF_LAT + row) * (COLS - HALF_LON)


def lon_row(array, level, row):
    return ((array * LEV + level) * (ROWS - HALF_LAT) + row) * HALF_LON


def cor_row(array, level, row):
    return ((array * LEV + level) * HALF_LAT + row) * HALF_LON


LAT_ROWS = lat_row(2, 0, 0)
LON_ROWS = lon_row(2, 0, 0)
COR_ROWS = cor_row(2, 0, 0)
KEEP_R = ROWS - HALF_LAT
KEEP_C = COLS - HALF_LON


def ff_kernel(
    first_hbm, second_hbm, cot_first_hbm, cot_second_hbm, gain_hbm, up_hbm, down_hbm,
    in_second_hbm, grad_first_hbm, x_ref, g_ref, lat_ref, lon_ref, cor_ref, gain_out_ref,
    hidden_ref, cot_up_ref, normed_ref, cot_ref,
    first_ref, second_ref, cot_first_ref, cot_second_ref, up_ref, down_ref,
    in_second_ref, grad_first_ref, gain_ref, in_sems, out_sems,
):
    sources = (first_hbm, up_hbm, cot_second_hbm, down_hbm, second_hbm, cot_first_hbm, gain_hbm)
    targets = (first_ref, up_ref, cot_second_ref, down_ref, second_ref, cot_first_ref, gain_ref)
    loads = [pltpu.make_async_copy(x, y, in_sems.at[i]) for i, (x, y) in enumerate(zip(sources, targets))]
    for load in loads:
        load.start()
    loads[0].wait()
    loads[6].wait()
    tokens = first_ref[...].reshape(TOKENS, D)
    gain = gain_ref[...]
    unit_field, inverse = norm_parts(tokens)
    normed_ref[...] = (unit_field * gain).astype(bf16)
    for load in loads[1:4]:
        load.wait()
    cot = cot_second_ref[...].astype(f32).reshape(TOKENS, D).astype(bf16)
    cot_ref[...] = cot
    w_up = up_ref[...]
    w_down_t = down_ref[...]
    step = 96
    for i in range(TOKENS // step):
        part = pl.ds(i * step, step)
        up_proj = nn(normed_ref[part, :], w_up)
        square = up_proj * up_proj
        half = 0.5 * (1.0 + jnp.tanh(up_proj * (gelu_scale + gelu_scale * gelu_cubic * square)))
        hidden_ref[part, :] = (up_proj * half).astype(bf16)
        cot_hidden = nn(cot[i * step : (i + 1) * step], w_down_t)
        slope = half + (half * (1.0 - half)) * up_proj * (
            2.0 * gelu_scale + 6.0 * gelu_scale * gelu_cubic * square
        )
        cot_up_ref[part, :] = (cot_hidden * slope).astype(bf16)
    hidden = hidden_ref[...]
    cot_up = cot_up_ref[...]
    shape = (LEV, ROWS, COLS, D)
    loads[4].wait()
    in_second_ref[...] = second_ref[...] - nt(hidden, w_down_t).reshape(shape)
    stores = [
        pltpu.make_async_copy(in_second_ref, in_second_hbm, out_sems.at[0]),
        pltpu.make_async_copy(grad_first_ref, grad_first_hbm, out_sems.at[1]),
    ]
    stores[0].start()
    cot_normed = nt(cot_up, w_up)
    gain_out_ref[...] = jnp.sum(cot_normed * unit_field, 0, keepdims=True)
    back = norm_back(cot_normed, gain, unit_field, inverse)
    loads[5].wait()
    grad_first_ref[...] = cot_first_ref[...].astype(f32) + back.reshape(shape)
    stores[1].start()
    for array, ref in enumerate((in_second_ref, grad_first_ref)):
        for level in range(LEV):
            for row in range(HALF_LAT):
                at = lat_row(array, level, row)
                lat_ref[at : at + KEEP_C, :] = ref[level, KEEP_R + row, 0:KEEP_C, :]
                at = cor_row(array, level, row)
                cor_ref[at : at + HALF_LON, :] = ref[level, KEEP_R + row, KEEP_C:COLS, :]
            for row in range(KEEP_R):
                at = lon_row(array, level, row)
                lon_ref[at : at + HALF_LON, :] = ref[level, row, KEEP_C:COLS, :]
    for at, count, source, level, line, start in all_pieces():
        if source == "own":
            x_ref[at : at + count, :] = in_second_ref[level, line, start : start + count, :]
            g_ref[at : at + count, :] = grad_first_ref[level, line, start : start + count, :]
    for store in stores:
        store.wait()


def ff_grads_kernel(normed_ref, cot_up_ref, cot_ref, hidden_ref, keep_ref, send_ref):
    grad_up = tn(normed_ref[...], cot_up_ref[...])
    grad_down = tn(cot_ref[...], hidden_ref[...])
    for k, grad in enumerate((grad_up, grad_down)):
        tiles = [grad[:, t * LANES : (t + 1) * LANES] for t in range(6)]
        halves = [jnp.concatenate(tiles[3 * h : 3 * h + 3], 0) for h in range(2)]
        mine = lat_bit(0) == 0
        kept = jnp.where(mine, halves[0], halves[1])
        sent = jnp.where(mine, halves[1], halves[0])
        for j in range(CHIPS):
            keep_ref[j, k * PART : (k + 1) * PART, :] = kept[j * PART : (j + 1) * PART]
            send_ref[j, k * PART : (k + 1) * PART, :] = sent[j * PART : (j + 1) * PART]


def window_of(band, level, sector):
    return (band * LEV + level) * SECTORS + sector


def pieces(band, sector):
    for row in range(WIN_LAT):
        rolled = band * WIN_LAT + row
        edge = rolled < HALF_LAT
        line = rolled if edge else rolled - HALF_LAT
        if sector == 0:
            yield row, 0, HALF_LON, "cor" if edge else "lon", line, 0
            yield row, HALF_LON, HALF_LON, "lat" if edge else "own", line, 0
        else:
            yield row, 0, WIN_LON, "lat" if edge else "own", line, HALF_LON


def strip_row(source, array, level, line, column):
    place = {"lat": lat_row, "lon": lon_row, "cor": cor_row}[source]
    return place(array, level, line) + column


def all_pieces():
    for band in range(BANDS):
        for level in range(LEV):
            initial = (level - LEV // 2) % LEV
            for sector in range(SECTORS):
                base = window_of(band, level, sector) * CELLS
                for row, col, count, source, line, start in pieces(band, sector):
                    yield base + row * WIN_LON + col, count, source, initial, line, start


def attention_kernel(
    x_in_ref, g_in_ref, lat_ref, lon_ref, cor_ref,
    bias_ref, gain_ref, qkv_ref, proj_ref,
    bias_keep_ref, bias_send_ref, x_ref, normed_ref, cot_low_ref, att16_ref, cq16_ref, ck16_ref, cv16_ref,
    g_ref, q_ref, k_ref, v_ref, ca_ref, att_ref, cq_ref, ck_ref, cv_ref,
):
    strips = {"lat": lat_ref, "lon": lon_ref, "cor": cor_ref}
    for at, count, source, level, line, start in all_pieces():
        for array, (dst, own) in enumerate(((x_ref, x_in_ref), (g_ref, g_in_ref))):
            if source == "own":
                dst[at : at + count, :] = own[at : at + count, :]
            else:
                src = strip_row(source, array, level, line, start)
                dst[at : at + count, :] = strips[source][src : src + count, :]
    gain = gain_ref[...]
    unit_field, inverse = norm_parts(x_ref[...])
    normed = (unit_field * gain).astype(bf16)
    weights_qkv = [qkv_ref[:, i * D : (i + 1) * D] for i in range(3)]
    w_proj = proj_ref[...]
    for ref, weight in zip((q_ref, k_ref, v_ref), weights_qkv):
        ref[...] = nn(normed, weight).astype(bf16).astype(f32)
    cot_low = g_ref[...].astype(bf16)
    ca_ref[...] = nt(cot_low, w_proj).astype(bf16).astype(f32)

    lane_head = lax.broadcasted_iota(jnp.int32, (CELLS, D), 1) // HEAD_DIM
    of_head = [lane_head == h for h in range(HEADS)]
    pad = jnp.zeros((LANES - CELLS, D), f32)

    def stacked(value):
        return jnp.concatenate([jnp.where(m, value, 0.0) for m in of_head], 0).astype(bf16)

    def gathered(value):
        total = jnp.where(of_head[0], value[:CELLS], 0.0)
        for h in range(1, HEADS):
            total = jnp.where(of_head[h], value[h * CELLS : (h + 1) * CELLS], total)
        return total

    first_band = lax.axis_index("lat") == 0
    query_low = lax.broadcasted_iota(jnp.int32, (CELLS, LANES), 0) < CELLS // 2
    key = lax.broadcasted_iota(jnp.int32, (CELLS, LANES), 1)
    apart = jnp.logical_and(query_low != (key < CELLS // 2), first_band)
    lane = lax.broadcasted_iota(jnp.int32, (STACK, LANES), 1)
    bias_grads = []
    for band in range(BANDS):
        for level in range(LEV):
            tables = []
            low = level * CELLS
            for h in range(HEADS):
                table = bias_ref[band, 0, h].astype(f32)[low : low + CELLS, low : low + CELLS]
                table = jnp.concatenate([table, jnp.full((CELLS, LANES - CELLS), padded_score, f32)], 1)
                if band == 0:
                    table = jnp.where(jnp.logical_and(apart, key < CELLS), masked_score, table)
                tables.append(table)
            table = jnp.concatenate(tables, 0)
            bias_grad = None
            for sector in range(SECTORS):
                base = window_of(band, level, sector) * CELLS
                part = slice(base, base + CELLS)
                queries = stacked(q_ref[part, :])
                key_part = jnp.concatenate([k_ref[part, :], pad], 0).astype(bf16)
                value_part = jnp.concatenate([v_ref[part, :], pad], 0).astype(bf16)
                scores = nt(queries, key_part) * score_scale + table
                exponent = jnp.exp(scores - jnp.max(scores, -1, keepdims=True))
                probability = exponent * (1.0 / jnp.sum(exponent, -1, keepdims=True))
                weights = probability.astype(bf16)
                att_ref[part, :] = gathered(nn(weights, value_part))
                cot_att = stacked(ca_ref[part, :])
                cot_weights = nt(cot_att, value_part)
                cv_ref[part, :] = tn(weights, cot_att)[:CELLS]
                inner = jnp.sum(cot_weights * probability, -1, keepdims=True)
                cot_scores = probability * (cot_weights - inner)
                bias_grad = cot_scores if bias_grad is None else bias_grad + cot_scores
                scaled = (cot_scores * score_scale).astype(bf16)
                cq_ref[part, :] = gathered(nn(scaled, key_part))
                ck_ref[part, :] = tn(scaled, queries)[:CELLS]
            bias_grads.append(bias_grad)
    left = [
        jnp.where(lane < 64, bias_grads[2 * b], pltpu.roll(bias_grads[2 * b + 1], 64, 1))
        for b in range(BANDS)
    ]
    lane3 = lane[: STACK // 3]
    rest = jnp.zeros((STACK // 3, LANES), f32)
    for g in range(3):
        for k in range(4):
            place = g * 32 + k * 8
            piece = bias_grads[k][g * (STACK // 3) : (g + 1) * (STACK // 3)]
            inside = jnp.logical_and(lane3 >= place, lane3 < place + 8)
            rest = jnp.where(inside, pltpu.roll(piece, (place - 64) % LANES, 1), rest)
    packed = jnp.concatenate([*left, rest, jnp.zeros((16, LANES), f32)], 0)
    packed = packed.reshape(2, 8, 64, LANES)
    for by, ref in ((1, bias_keep_ref), (3, bias_send_ref)):
        ref[...] = jnp.where(half_at(by) == 0, packed[0], packed[1])

    normed_ref[...] = normed
    cot_low_ref[...] = cot_low
    for src, dst in ((att_ref, att16_ref), (cq_ref, cq16_ref), (ck_ref, ck16_ref), (cv_ref, cv16_ref)):
        dst[...] = src[...].astype(bf16)


def attention_grads_kernel(
    x_ref, normed_ref, cot_low_ref, att16_ref, cq_ref, ck_ref, cv_ref, qkv_ref, gain_mlp_ref,
    keep_ref, send_ref, cot_normed_ref,
):
    unit_field, _ = norm_parts(x_ref[...])
    normed = normed_ref[...]
    grads = []
    cot_normed = None
    for i, ref in enumerate((cq_ref, ck_ref, cv_ref)):
        weight = qkv_ref[:, i * D : (i + 1) * D]
        cot_part = ref[...]
        grads.append(tn(normed, cot_part))
        term = nt(cot_part, weight)
        cot_normed = term if cot_normed is None else cot_normed + term
    grads.append(tn(att16_ref[...], cot_low_ref[...]))
    gain_part = jnp.sum(cot_normed * unit_field, 0, keepdims=True)
    cot_normed_ref[...] = cot_normed
    tiles = [g[:, :LANES] for g in grads]
    tiles += [jnp.concatenate([grads[i][:, LANES:], grads[i + 1][:, LANES:]], 1) for i in (0, 2)]
    halves = [jnp.concatenate(tiles[3 * h : 3 * h + 3], 0) for h in range(2)]
    mine = lat_bit(0) == 0
    kept = jnp.where(mine, halves[0], halves[1])
    sent = jnp.where(mine, halves[1], halves[0])
    gains = jnp.concatenate([gain_mlp_ref[...], gain_part], 0)
    right = jnp.concatenate([gains[:, LANES:], jnp.zeros((2, LANES - 64), f32)], 1)
    block = jnp.concatenate([gains[:, :LANES], right], 0)
    for ref, half in ((keep_ref, kept), (send_ref, sent)):
        for j in range(CHIPS):
            ref[j, :PART, :] = half[j * PART : (j + 1) * PART]
            ref[j, PART:, :] = block


def return_kernel(
    x_ref, att16_ref, cot_normed_ref, gain_ref, proj_ref,
    win_f_hbm, win_c_hbm, out_lat_ref, out_lon_ref, out_cor_ref,
    win_f_ref, win_c_ref, sems,
):
    win_f_ref[...] = nn(att16_ref[...], proj_ref[...])
    unit_field, inverse = norm_parts(x_ref[...])
    win_c_ref[...] = norm_back(cot_normed_ref[...], gain_ref[...], unit_field, inverse)
    stores = [
        pltpu.make_async_copy(win_f_ref, win_f_hbm, sems.at[0]),
        pltpu.make_async_copy(win_c_ref, win_c_hbm, sems.at[1]),
    ]
    for store in stores:
        store.start()
    out_strips = {"lat": out_lat_ref, "lon": out_lon_ref, "cor": out_cor_ref}
    for at, count, source, level, line, start in all_pieces():
        if source != "own":
            for array, src in enumerate((win_f_ref, win_c_ref)):
                dst = strip_row(source, array, level, line, start)
                out_strips[source][dst : dst + count, :] = src[at : at + count, :]
    for store in stores:
        store.wait()


def halve_kernel(bit, keep_ref, recv_ref, keep_out_ref, send_out_ref):
    total = keep_ref[...] + recv_ref[...]
    inner = {"x_low": 4, "y_low": 1, "y_high": 1, "x_high": 1}[bit]
    total = total.reshape(-1, 2, inner, *total.shape[1:])
    low, high = (total[:, i].reshape(keep_out_ref.shape) for i in range(2))
    own = {"x_low": lambda: lat_bit(3), "y_low": lambda: lat_bit(1), "y_high": lambda: lat_bit(2),
           "x_high": lambda: lax.axis_index("lon") // 8}[bit]()
    keep_out_ref[...] = jnp.where(own == 0, low, high)
    send_out_ref[...] = jnp.where(own == 0, high, low)


def xy_join_kernel(keep_ref, recv_ref, out_ref):
    out_ref[...] = keep_ref[...] + recv_ref[...]


def z_join_kernel(bias_ref, recv_ref, parts_ref, ff_ref, ff_recv_ref, out_ref):
    weights = jnp.concatenate(
        [ff_ref[0] + ff_recv_ref[0], jnp.sum(parts_ref[...], 0), jnp.zeros((16, LANES), f32)], 0
    )
    out_ref[:, :64, :] = bias_ref[...] + recv_ref[...]
    out_ref[:, 64:, :] = weights.reshape(8, 16, LANES)


def total_kernel(in_ref, out_ref):
    out_ref[...] = jnp.broadcast_to(jnp.sum(in_ref[...], 0)[None], out_ref.shape)


def spread_kernel(in_ref, out_ref, bias_ref):
    weights = in_ref[:, 64:, :].reshape(128, LANES)
    out_ref[...] = jnp.broadcast_to(weights[None, : 3 * PART + 4], out_ref.shape)
    bias_ref[...] = in_ref[:, :64, :]


def bias_kernel(next_ref, before_ref, bias_ref):
    first = half_at(1) == 0
    after, before = (ref[...].reshape(512, LANES) for ref in (next_ref, before_ref))
    packed = jnp.concatenate([jnp.where(first, after, before), jnp.where(first, before, after)], 0)
    lane = lax.broadcasted_iota(jnp.int32, (STACK, LANES), 1)
    third = STACK // 3
    rest = packed[2 * STACK : 2 * STACK + third]
    zeros = jnp.zeros((CELLS, LANES), f32)
    for band in range(BANDS):
        for level in range(LEV):
            table = packed[band * STACK : (band + 1) * STACK]
            if level == 1:
                table = pltpu.roll(table, 64, 1)
            k = band * LEV + level
            tail = jnp.concatenate([pltpu.roll(rest, (64 - g * 32 - k * 8) % LANES, 1) for g in range(3)], 0)
            table = jnp.where(lane < 64, table, jnp.where(lane < CELLS, tail, 0.0))
            for h in range(HEADS):
                rows = jnp.concatenate([table[h * CELLS : (h + 1) * CELLS], zeros], 1)
                if level == 1:
                    rows = pltpu.roll(rows, CELLS, 1)
                bias_ref[band, 0, h, level * CELLS : (level + 1) * CELLS, :] = rows[:, : 2 * CELLS]


def last_kernel(
    mine_ref, other_ref,
    gain_attn_ref, qkv_ref, proj_ref, gain_mlp_ref, up_ref, down_ref, rows_ref,
):
    gains = mine_ref[0, 3 * PART :, :]
    gains = jnp.concatenate([gains[:2], gains[2:4, :64]], 1)
    gain_mlp_ref[...] = gains[0:1]
    gain_attn_ref[...] = gains[1:2]
    own = lat_bit(0) == 0

    def tiles_of(k):
        found = []
        for low in (True, False):
            for j in range(CHIPS):
                mine, other = (ref[j, k * PART : (k + 1) * PART, :] for ref in (mine_ref, other_ref))
                rows_ref[j * PART : (j + 1) * PART, :] = jnp.where(own, mine, other) if low else jnp.where(own, other, mine)
            found += [rows_ref[t * D : (t + 1) * D, :] for t in range(3)]
        return found

    tiles = tiles_of(2)
    parts = [
        jnp.concatenate([tiles[i], tiles[4 + i // 2][:, 64 * (i % 2) : 64 * (i % 2) + 64]], 1)
        for i in range(4)
    ]
    qkv_ref[...] = jnp.concatenate(parts[:3], 1)
    proj_ref[...] = parts[3]
    up_ref[...] = jnp.concatenate(tiles_of(0), 1)
    down_ref[...] = jnp.concatenate(tiles_of(1), 1)


def stream_kernel(
    first_ref, cot_second_ref, win_f_hbm, win_c_hbm, lat_ref, lon_ref, cor_ref,
    in_first_ref, grad_second_ref, cot_ref, win_f_ref, win_c_ref, sems,
):
    loads = [
        pltpu.make_async_copy(win_f_hbm, win_f_ref, sems.at[0]),
        pltpu.make_async_copy(win_c_hbm, win_c_ref, sems.at[1]),
    ]
    for load in loads:
        load.start()
    cot_ref[...] = cot_second_ref[...].astype(f32)
    for load in loads:
        load.wait()
    strips = {"lat": lat_ref, "lon": lon_ref, "cor": cor_ref}
    for at, count, source, level, line, start in all_pieces():
        if source == "own":
            f_part, c_part = (ref[at : at + count, :] for ref in (win_f_ref, win_c_ref))
            row, col = line, start
        else:
            row = line + (0 if source == "lon" else KEEP_R)
            col = start + (0 if source == "lat" else KEEP_C)
            at_f, at_c = (strip_row(source, array, level, line, start) for array in range(2))
            f_part, c_part = (strips[source][p : p + count, :] for p in (at_f, at_c))
        spot = (level, row, slice(col, col + count))
        in_first_ref[spot] = first_ref[spot] - f_part
        grad_second_ref[spot] = cot_ref[spot] + c_part


def kernel(fn, out_shape, scratch=(), name=None, flops=0, nbytes=0, in_hbm=(), out_hbm=()):
    def spec(far):
        return pl.BlockSpec(memory_space=pltpu.HBM if far else pltpu.VMEM)

    def in_specs(count):
        return [spec(i in in_hbm) for i in range(count)]

    def call(*args):
        args = [
            pltpu.with_memory_space_constraint(x, pltpu.HBM) if i in in_hbm else x
            for i, x in enumerate(args)
        ]
        return pl.pallas_call(
            fn,
            out_shape=[s if hasattr(s, "dtype") else jax.ShapeDtypeStruct(s, f32) for s in out_shape],
            in_specs=in_specs(len(args)),
            out_specs=[spec(i in out_hbm) for i in range(len(out_shape))],
            scratch_shapes=[s if not isinstance(s, tuple) else pltpu.VMEM(*s) for s in scratch],
            compiler_params=pltpu.CompilerParams(vmem_limit_bytes=32 * 1024 * 1024),
            cost_estimate=pl.CostEstimate(flops=flops, bytes_accessed=nbytes, transcendentals=0),
            name=name,
        )(*args)

    return call


def body(
    out_first, out_second, cot_first, cot_second,
    gain_attn, w_qkv, w_proj, earth_bias, gain_mlp, w_up, w_down,
):
    lat_count, lon_count = lax.axis_size("lat"), lax.axis_size("lon")
    both = ("lat", "lon")
    shape = (LEV, ROWS, COLS, D)

    def halo(lat, lon, cor, by):
        ring = lambda n: [(i, (i + by) % n) for i in range(n)]
        diagonal = [
            (a * lon_count + o, ((a + by) % lat_count) * lon_count + (o + by) % lon_count)
            for a in range(lat_count)
            for o in range(lon_count)
        ]
        return (
            lax.ppermute(lat, "lat", ring(lat_count)),
            lax.ppermute(lon, "lon", ring(lon_count)),
            lax.ppermute(cor, both, diagonal),
        )

    same_z = [
        [(2 * chip + core) * lon_count + x * 8 + z for x in range(2) for chip in range(8)]
        for core in range(2)
        for z in range(8)
    ]
    same_x = [list(range(8)), list(range(8, 16))]

    def swap_xy(value):
        return lax.all_to_all(value, both, 0, 0, tiled=True, axis_index_groups=same_z)

    def swap_z(value):
        return lax.all_to_all(value, "lon", 0, 0, tiled=True, axis_index_groups=same_x)

    def across_x(value):
        return lax.ppermute(value, "lon", [(i, i ^ 8) for i in range(lon_count)])

    def along_x(value, by):
        def there(a, o):
            x = (o // 8 * 2 + a // 8 + by) % 4
            return (x % 2 * 8 + a % 8) * lon_count + x // 2 * 8 + o % 8

        pairs = [(a * lon_count + o, there(a, o)) for a in range(lat_count) for o in range(lon_count)]
        return lax.ppermute(value, both, pairs)

    def across(value, bit):
        return lax.ppermute(value, "lat", [(i, i ^ (1 << bit)) for i in range(lat_count)])

    strip_shapes = [(LAT_ROWS, D), (LON_ROWS, D), (COR_ROWS, D)]
    win = (TOKENS, D)
    ff_half = (CHIPS, 2 * PART, LANES)
    half_bytes = lambda *dims: jax.ShapeDtypeStruct(dims, bf16)
    (
        in_second, grad_first, x_win, g_win, lat, lon, cor, gain_mlp_part, hidden, cot_up, normed, cot,
    ) = kernel(
        ff_kernel,
        [
            shape, shape, win, win, *strip_shapes, (1, D),
            half_bytes(TOKENS, FF), half_bytes(TOKENS, FF), half_bytes(TOKENS, D), half_bytes(TOKENS, D),
        ],
        [
            (shape, f32), (shape, f32), (shape, bf16), (shape, bf16), ((D, FF), bf16), ((D, FF), bf16),
            (shape, f32), (shape, f32), ((1, D), f32),
            pltpu.SemaphoreType.DMA((7,)), pltpu.SemaphoreType.DMA((2,)),
        ],
        "feedforward",
        flops=8 * TOKENS * D * FF,
        nbytes=6_000_000,
        in_hbm=tuple(range(7)),
        out_hbm=(0, 1),
    )(out_first, out_second, cot_first, cot_second, gain_mlp.reshape(1, D), w_up, w_down.T)
    lat, lon, cor = halo(lat, lon, cor, 1)
    ff_keep, ff_send = kernel(
        ff_grads_kernel, [ff_half, ff_half], name="ffgrads", flops=2_000_000_000, nbytes=4_000_000
    )(normed, cot_up, cot, hidden)
    def ff_step(bit, keep, recv):
        parts = (keep.shape[0] // 2, *keep.shape[1:])
        return kernel(functools.partial(halve_kernel, bit), [parts, parts], name="halve")(keep, recv)

    ff_keep, ff_send = ff_step("x_low", ff_keep, across(ff_send, 0))
    x_win, ff_keep, ff_send = lax.optimization_barrier((x_win, ff_keep, ff_send))
    ff_recv = across(ff_send, 3)
    at_half = (CHIPS, PART + 4, LANES)
    bias_half = (8, 64, LANES)
    gain = gain_attn.reshape(1, D)
    half_win = half_bytes(*win)
    bias_keep, bias_send, x_win, *attention_parts = kernel(
        attention_kernel,
        [bias_half, bias_half, win, *[half_win] * 6],
        [(win, f32)] * 9,
        "attention",
        flops=14_000_000_000,
        nbytes=16_000_000,
    )(x_win, g_win, lat, lon, cor, earth_bias, gain, w_qkv, w_proj)
    bias_keep, bias_recv = along_x(bias_keep, 1), along_x(bias_send, -1)
    keep, send, cot_normed = kernel(
        attention_grads_kernel, [at_half, at_half, win], name="attngrads", flops=2_000_000_000, nbytes=4_000_000
    )(x_win, *attention_parts, w_qkv, gain_mlp_part)
    attended = attention_parts[2]
    keep, send, x_win, ff_recv = lax.optimization_barrier((keep, send, x_win, ff_recv))
    ff_keep, ff_send = ff_step("y_low", ff_keep, ff_recv)
    ff_keep, ff_send = ff_step("y_high", ff_keep, across(ff_send, 1))
    ff_recv = across(ff_send, 2)
    win_f, win_c, lat, lon, cor = kernel(
        return_kernel,
        [win, win, *strip_shapes],
        [(win, f32), (win, f32), pltpu.SemaphoreType.DMA((2,))],
        "returns",
        flops=1_000_000_000,
        nbytes=4_000_000,
        out_hbm=(0, 1),
    )(x_win, attended, cot_normed, gain, w_proj)
    recv, win_f, win_c, lat, lon, cor = lax.optimization_barrier(
        (across(send, 0), win_f, win_c, lat, lon, cor)
    )
    lat, lon, cor = halo(lat, lon, cor, -1)
    block = (CHIPS, 3 * PART + 4, LANES)
    (parts,) = kernel(xy_join_kernel, [at_half], name="xyjoin")(keep, recv)
    parts, bias_keep, bias_recv, ff_recv = lax.optimization_barrier((parts, bias_keep, bias_recv, ff_recv))
    ff_keep, ff_send = ff_step("x_high", ff_keep, ff_recv)
    ff_recv = across_x(ff_send)
    parts = swap_xy(parts)
    (joined,) = kernel(z_join_kernel, [(8, 80, LANES)], name="zjoin")(
        bias_keep, bias_recv, parts, ff_keep, ff_recv
    )
    joined = swap_z(joined)
    (totals,) = kernel(total_kernel, [(8, 80, LANES)], name="total")(joined)
    totals = swap_z(totals)
    spread, bias_mine = kernel(spread_kernel, [block, bias_half], name="spread")(totals)
    bias_mine, bias_other = along_x(bias_mine, -1), along_x(bias_mine, 1)
    mine = swap_xy(spread)
    mine, lat, lon, cor = lax.optimization_barrier((mine, lat, lon, cor))
    in_first, grad_second = kernel(
        stream_kernel,
        [shape, shape],
        [(shape, f32), (win, f32), (win, f32), pltpu.SemaphoreType.DMA((2,))],
        "streams",
        nbytes=3_000_000,
        flops=2_000_000_000,
        in_hbm=(2, 3),
    )(out_first, cot_second, win_f, win_c, lat, lon, cor)
    mine, bias_mine, bias_other = lax.optimization_barrier((mine, bias_mine, bias_other))
    other = across(mine, 0)
    (grad_bias,) = kernel(bias_kernel, [(BANDS, 1, HEADS, 2 * CELLS, 2 * CELLS)], name="bias")(
        bias_mine, bias_other
    )
    grad_gain_attn, grad_qkv, grad_proj, grad_gain_mlp, grad_up, grad_down = kernel(
        last_kernel,
        [(1, D), (D, 3 * D), (D, D), (1, D), (D, FF), (D, FF)],
        [((3 * D, LANES), f32)],
        name="last",
        nbytes=6_000_000,
    )(mine, other)
    return (
        in_first, in_second, grad_first, grad_second,
        grad_gain_attn.reshape(D), grad_qkv, grad_proj, grad_bias,
        grad_gain_mlp.reshape(D), grad_up, grad_down.T,
    )


def solution(mesh):
    field = P(None, "lat", "lon", None)
    placed = (field,) * 4 + (P(), P(), P(), P("lat", None, None, None, None), P(), P(), P())
    return jax.shard_map(body, mesh=mesh, in_specs=placed, out_specs=placed, check_vma=False)
```

```python
import functools

import jax
import jax.numpy as jnp
from jax import lax
from jax.experimental import pallas as pl
from jax.experimental.pallas import tpu as pltpu
from jax.sharding import PartitionSpec as P

HEADS = 6
HEAD_DIM = 32
D = 192
FF = 768
LEV = 2
WIN_LAT = 6
WIN_LON = 12
CELLS = WIN_LAT * WIN_LON
BANDS = 2
CHIPS = 16
PART = 3 * 192 // 16
SECTORS = 2
ROWS = BANDS * WIN_LAT
COLS = SECTORS * WIN_LON
TOKENS = LEV * ROWS * COLS
HALF_LAT = WIN_LAT // 2
HALF_LON = WIN_LON // 2
STACK = HEADS * CELLS
LANES = 128

norm_eps = 1e-05
gelu_scale = 0.7978845608028654
gelu_cubic = 0.044715
masked_score = -1000000000.0
padded_score = -1e30
score_scale = HEAD_DIM ** (-0.5)

f32 = jnp.float32
bf16 = jnp.bfloat16


def nn(a, b):
    return lax.dot_general(a, b, (((1,), (0,)), ((), ())), preferred_element_type=f32)


def nt(a, b):
    return lax.dot_general(a, b, (((1,), (1,)), ((), ())), preferred_element_type=f32)


def tn(a, b):
    return lax.dot_general(a, b, (((0,), (0,)), ((), ())), preferred_element_type=f32)


def norm_parts(field):
    average = jnp.mean(field, -1, keepdims=True)
    centred = field - average
    inverse = lax.rsqrt(jnp.mean(centred * centred, -1, keepdims=True) + norm_eps)
    return (centred * inverse, inverse)


def norm_back(cot_normed, norm_gain, unit_field, inverse):
    cot_unit = cot_normed * norm_gain
    return inverse * (
        cot_unit
        - jnp.mean(cot_unit, -1, keepdims=True)
        - unit_field * jnp.mean(cot_unit * unit_field, -1, keepdims=True)
    )


def half_at(by):
    x = lax.axis_index("lon") // 8 * 2 + lax.axis_index("lat") // 8
    return lax.rem(x + by, 4) // 2


def lat_bit(k):
    return lax.rem(lax.axis_index("lat") // (1 << k), 2)


def lat_row(array, level, row):
    return ((array * LEV + level) * HALF_LAT + row) * (COLS - HALF_LON)


def lon_row(array, level, row):
    return ((array * LEV + level) * (ROWS - HALF_LAT) + row) * HALF_LON


def cor_row(array, level, row):
    return ((array * LEV + level) * HALF_LAT + row) * HALF_LON


LAT_ROWS = lat_row(2, 0, 0)
LON_ROWS = lon_row(2, 0, 0)
COR_ROWS = cor_row(2, 0, 0)
KEEP_R = ROWS - HALF_LAT
KEEP_C = COLS - HALF_LON


def ff_kernel(
    first_hbm, second_hbm, cot_first_hbm, cot_second_hbm, gain_hbm, up_hbm, down_hbm,
    in_second_hbm, grad_first_hbm, x_ref, g_ref, lat_ref, lon_ref, cor_ref, gain_out_ref,
    hidden_ref, cot_up_ref, normed_ref, cot_ref,
    first_ref, second_ref, cot_first_ref, cot_second_ref, up_ref, down_ref,
    in_second_ref, grad_first_ref, gain_ref, in_sems, out_sems,
):
    sources = (first_hbm, up_hbm, cot_second_hbm, down_hbm, second_hbm, cot_first_hbm, gain_hbm)
    targets = (first_ref, up_ref, cot_second_ref, down_ref, second_ref, cot_first_ref, gain_ref)
    loads = [pltpu.make_async_copy(x, y, in_sems.at[i]) for i, (x, y) in enumerate(zip(sources, targets))]
    for load in loads:
        load.start()
    loads[0].wait()
    loads[6].wait()
    tokens = first_ref[...].reshape(TOKENS, D)
    gain = gain_ref[...]
    unit_field, inverse = norm_parts(tokens)
    normed_ref[...] = (unit_field * gain).astype(bf16)
    for load in loads[1:4]:
        load.wait()
    cot = cot_second_ref[...].astype(f32).reshape(TOKENS, D).astype(bf16)
    cot_ref[...] = cot
    w_up = up_ref[...]
    w_down_t = down_ref[...]
    step = 96
    for i in range(TOKENS // step):
        part = pl.ds(i * step, step)
        up_proj = nn(normed_ref[part, :], w_up)
        square = up_proj * up_proj
        half = 0.5 * (1.0 + jnp.tanh(up_proj * (gelu_scale + gelu_scale * gelu_cubic * square)))
        hidden_ref[part, :] = (up_proj * half).astype(bf16)
        cot_hidden = nn(cot[i * step : (i + 1) * step], w_down_t)
        slope = half + (half * (1.0 - half)) * up_proj * (
            2.0 * gelu_scale + 6.0 * gelu_scale * gelu_cubic * square
        )
        cot_up_ref[part, :] = (cot_hidden * slope).astype(bf16)
    hidden = hidden_ref[...]
    cot_up = cot_up_ref[...]
    shape = (LEV, ROWS, COLS, D)
    loads[4].wait()
    in_second_ref[...] = second_ref[...] - nt(hidden, w_down_t).reshape(shape)
    stores = [
        pltpu.make_async_copy(in_second_ref, in_second_hbm, out_sems.at[0]),
        pltpu.make_async_copy(grad_first_ref, grad_first_hbm, out_sems.at[1]),
    ]
    stores[0].start()
    cot_normed = nt(cot_up, w_up)
    gain_out_ref[...] = jnp.sum(cot_normed * unit_field, 0, keepdims=True)
    back = norm_back(cot_normed, gain, unit_field, inverse)
    loads[5].wait()
    grad_first_ref[...] = cot_first_ref[...].astype(f32) + back.reshape(shape)
    stores[1].start()
    for array, ref in enumerate((in_second_ref, grad_first_ref)):
        for level in range(LEV):
            for row in range(HALF_LAT):
                at = lat_row(array, level, row)
                lat_ref[at : at + KEEP_C, :] = ref[level, KEEP_R + row, 0:KEEP_C, :]
                at = cor_row(array, level, row)
                cor_ref[at : at + HALF_LON, :] = ref[level, KEEP_R + row, KEEP_C:COLS, :]
            for row in range(KEEP_R):
                at = lon_row(array, level, row)
                lon_ref[at : at + HALF_LON, :] = ref[level, row, KEEP_C:COLS, :]
    for at, count, source, level, line, start in all_pieces():
        if source == "own":
            x_ref[at : at + count, :] = in_second_ref[level, line, start : start + count, :]
            g_ref[at : at + count, :] = grad_first_ref[level, line, start : start + count, :]
    for store in stores:
        store.wait()


def ff_grads_kernel(normed_ref, cot_up_ref, cot_ref, hidden_ref, keep_ref, send_ref):
    grad_up = tn(normed_ref[...], cot_up_ref[...])
    grad_down = tn(cot_ref[...], hidden_ref[...])
    for k, grad in enumerate((grad_up, grad_down)):
        tiles = [grad[:, t * LANES : (t + 1) * LANES] for t in range(6)]
        halves = [jnp.concatenate(tiles[3 * h : 3 * h + 3], 0) for h in range(2)]
        mine = lat_bit(0) == 0
        kept = jnp.where(mine, halves[0], halves[1])
        sent = jnp.where(mine, halves[1], halves[0])
        for j in range(CHIPS):
            keep_ref[j, k * PART : (k + 1) * PART, :] = kept[j * PART : (j + 1) * PART]
            send_ref[j, k * PART : (k + 1) * PART, :] = sent[j * PART : (j + 1) * PART]


def window_of(band, level, sector):
    return (band * LEV + level) * SECTORS + sector


def pieces(band, sector):
    for row in range(WIN_LAT):
        rolled = band * WIN_LAT + row
        edge = rolled < HALF_LAT
        line = rolled if edge else rolled - HALF_LAT
        if sector == 0:
            yield row, 0, HALF_LON, "cor" if edge else "lon", line, 0
            yield row, HALF_LON, HALF_LON, "lat" if edge else "own", line, 0
        else:
            yield row, 0, WIN_LON, "lat" if edge else "own", line, HALF_LON


def strip_row(source, array, level, line, column):
    place = {"lat": lat_row, "lon": lon_row, "cor": cor_row}[source]
    return place(array, level, line) + column


def all_pieces():
    for band in range(BANDS):
        for level in range(LEV):
            initial = (level - LEV // 2) % LEV
            for sector in range(SECTORS):
                base = window_of(band, level, sector) * CELLS
                for row, col, count, source, line, start in pieces(band, sector):
                    yield base + row * WIN_LON + col, count, source, initial, line, start


lane_head = lambda: lax.broadcasted_iota(jnp.int32, (CELLS, D), 1) // HEAD_DIM


def bias_table(bias_ref, band, level):
    query_low = lax.broadcasted_iota(jnp.int32, (CELLS, LANES), 0) < CELLS // 2
    key = lax.broadcasted_iota(jnp.int32, (CELLS, LANES), 1)
    first_band = lax.axis_index("lat") == 0
    apart = jnp.logical_and(query_low != (key < CELLS // 2), first_band)
    tables = []
    low = level * CELLS
    for h in range(HEADS):
        table = bias_ref[band, 0, h].astype(f32)[low : low + CELLS, low : low + CELLS]
        table = jnp.concatenate([table, jnp.full((CELLS, LANES - CELLS), padded_score, f32)], 1)
        if band == 0:
            table = jnp.where(jnp.logical_and(apart, key < CELLS), masked_score, table)
        tables.append(table)
    return jnp.concatenate(tables, 0)


def attend(query, key, value, cot_attended, table):
    heads = lane_head()
    of_head = [heads == h for h in range(HEADS)]
    pad = jnp.zeros((LANES - CELLS, D), f32)

    def stacked(value):
        return jnp.concatenate([jnp.where(m, value, 0.0) for m in of_head], 0).astype(bf16)

    def gathered(value):
        total = jnp.where(of_head[0], value[:CELLS], 0.0)
        for h in range(1, HEADS):
            total = jnp.where(of_head[h], value[h * CELLS : (h + 1) * CELLS], total)
        return total

    queries = stacked(query)
    key_part = jnp.concatenate([key, pad], 0).astype(bf16)
    value_part = jnp.concatenate([value, pad], 0).astype(bf16)
    scores = nt(queries, key_part) * score_scale + table
    exponent = jnp.exp(scores - jnp.max(scores, -1, keepdims=True))
    probability = exponent * (1.0 / jnp.sum(exponent, -1, keepdims=True))
    weights = probability.astype(bf16)
    attended = gathered(nn(weights, value_part))
    cot_att = stacked(cot_attended)
    cot_weights = nt(cot_att, value_part)
    cot_value = tn(weights, cot_att)[:CELLS]
    inner = jnp.sum(cot_weights * probability, -1, keepdims=True)
    cot_scores = probability * (cot_weights - inner)
    scaled = (cot_scores * score_scale).astype(bf16)
    cot_query = gathered(nn(scaled, key_part))
    cot_key = tn(scaled, queries)[:CELLS]
    return (attended, cot_query, cot_key, cot_value), cot_scores


def inner_attention_kernel(
    x_ref, g_ref, bias_ref, gain_ref, qkv_ref, proj_ref,
    att_ref, cq_ref, ck_ref, cv_ref, cot_scores_ref,
    q_ref, k_ref, v_ref, ca_ref,
):
    rows = [window_of(BANDS - 1, level, SECTORS - 1) * CELLS for level in range(LEV)]
    x, g = (jnp.concatenate([ref[at : at + CELLS, :] for at in rows], 0) for ref in (x_ref, g_ref))
    unit_field, _ = norm_parts(x)
    normed = (unit_field * gain_ref[...]).astype(bf16)
    for i, ref in enumerate((q_ref, k_ref, v_ref)):
        ref[...] = nn(normed, qkv_ref[:, i * D : (i + 1) * D]).astype(bf16).astype(f32)
    ca_ref[...] = nt(g.astype(bf16), proj_ref[...]).astype(bf16).astype(f32)
    for level in range(LEV):
        part = slice(level * CELLS, (level + 1) * CELLS)
        found, cot_scores = attend(
            q_ref[part, :], k_ref[part, :], v_ref[part, :], ca_ref[part, :],
            bias_table(bias_ref, BANDS - 1, level),
        )
        for ref, value in zip((att_ref, cq_ref, ck_ref, cv_ref), found):
            ref[part, :] = value
        cot_scores_ref[level] = cot_scores


def attention_kernel(
    x_in_ref, g_in_ref, lat_ref, lon_ref, cor_ref,
    bias_ref, gain_ref, qkv_ref, proj_ref,
    in_att_ref, in_cq_ref, in_ck_ref, in_cv_ref, in_cot_scores_ref,
    bias_keep_ref, bias_send_ref, x_ref, normed_ref, cot_low_ref, att16_ref, cq16_ref, ck16_ref, cv16_ref,
    g_ref, q_ref, k_ref, v_ref, ca_ref, att_ref, cq_ref, ck_ref, cv_ref,
):
    strips = {"lat": lat_ref, "lon": lon_ref, "cor": cor_ref}
    for at, count, source, level, line, start in all_pieces():
        for array, (dst, own) in enumerate(((x_ref, x_in_ref), (g_ref, g_in_ref))):
            if source == "own":
                dst[at : at + count, :] = own[at : at + count, :]
            else:
                src = strip_row(source, array, level, line, start)
                dst[at : at + count, :] = strips[source][src : src + count, :]
    unit_field, _ = norm_parts(x_ref[...])
    normed = (unit_field * gain_ref[...]).astype(bf16)
    for i, ref in enumerate((q_ref, k_ref, v_ref)):
        ref[...] = nn(normed, qkv_ref[:, i * D : (i + 1) * D]).astype(bf16).astype(f32)
    cot_low = g_ref[...].astype(bf16)
    ca_ref[...] = nt(cot_low, proj_ref[...]).astype(bf16).astype(f32)
    lane = lax.broadcasted_iota(jnp.int32, (STACK, LANES), 1)
    bias_grads = []
    for band in range(BANDS):
        for level in range(LEV):
            table = bias_table(bias_ref, band, level)
            bias_grad = None
            for sector in range(SECTORS):
                base = window_of(band, level, sector) * CELLS
                part = slice(base, base + CELLS)
                if band == BANDS - 1 and sector == SECTORS - 1:
                    given = slice(level * CELLS, (level + 1) * CELLS)
                    found = tuple(ref[given, :] for ref in (in_att_ref, in_cq_ref, in_ck_ref, in_cv_ref))
                    cot_scores = in_cot_scores_ref[level]
                else:
                    found, cot_scores = attend(
                        q_ref[part, :], k_ref[part, :], v_ref[part, :], ca_ref[part, :], table
                    )
                for ref, value in zip((att_ref, cq_ref, ck_ref, cv_ref), found):
                    ref[part, :] = value
                bias_grad = cot_scores if bias_grad is None else bias_grad + cot_scores
            bias_grads.append(bias_grad)
    left = [
        jnp.where(lane < 64, bias_grads[2 * b], pltpu.roll(bias_grads[2 * b + 1], 64, 1))
        for b in range(BANDS)
    ]
    lane3 = lane[: STACK // 3]
    rest = jnp.zeros((STACK // 3, LANES), f32)
    for g in range(3):
        for k in range(4):
            place = g * 32 + k * 8
            piece = bias_grads[k][g * (STACK // 3) : (g + 1) * (STACK // 3)]
            inside = jnp.logical_and(lane3 >= place, lane3 < place + 8)
            rest = jnp.where(inside, pltpu.roll(piece, (place - 64) % LANES, 1), rest)
    packed = jnp.concatenate([*left, rest, jnp.zeros((16, LANES), f32)], 0)
    packed = packed.reshape(2, 8, 64, LANES)
    for by, ref in ((1, bias_keep_ref), (3, bias_send_ref)):
        ref[...] = jnp.where(half_at(by) == 0, packed[0], packed[1])

    normed_ref[...] = normed
    cot_low_ref[...] = cot_low
    for src, dst in ((att_ref, att16_ref), (cq_ref, cq16_ref), (ck_ref, ck16_ref), (cv_ref, cv16_ref)):
        dst[...] = src[...].astype(bf16)


def attention_grads_kernel(
    x_ref, normed_ref, cot_low_ref, att16_ref, cq_ref, ck_ref, cv_ref, qkv_ref, gain_mlp_ref,
    keep_ref, send_ref, cot_normed_ref,
):
    unit_field, _ = norm_parts(x_ref[...])
    normed = normed_ref[...]
    grads = []
    cot_normed = None
    for i, ref in enumerate((cq_ref, ck_ref, cv_ref)):
        weight = qkv_ref[:, i * D : (i + 1) * D]
        cot_part = ref[...]
        grads.append(tn(normed, cot_part))
        term = nt(cot_part, weight)
        cot_normed = term if cot_normed is None else cot_normed + term
    grads.append(tn(att16_ref[...], cot_low_ref[...]))
    gain_part = jnp.sum(cot_normed * unit_field, 0, keepdims=True)
    cot_normed_ref[...] = cot_normed
    tiles = [g[:, :LANES] for g in grads]
    tiles += [jnp.concatenate([grads[i][:, LANES:], grads[i + 1][:, LANES:]], 1) for i in (0, 2)]
    halves = [jnp.concatenate(tiles[3 * h : 3 * h + 3], 0) for h in range(2)]
    mine = lat_bit(0) == 0
    kept = jnp.where(mine, halves[0], halves[1])
    sent = jnp.where(mine, halves[1], halves[0])
    gains = jnp.concatenate([gain_mlp_ref[...], gain_part], 0)
    right = jnp.concatenate([gains[:, LANES:], jnp.zeros((2, LANES - 64), f32)], 1)
    block = jnp.concatenate([gains[:, :LANES], right], 0)
    for ref, half in ((keep_ref, kept), (send_ref, sent)):
        for j in range(CHIPS):
            ref[j, :PART, :] = half[j * PART : (j + 1) * PART]
            ref[j, PART:, :] = block


def return_kernel(
    x_ref, att16_ref, cot_normed_ref, gain_ref, proj_ref,
    win_f_hbm, win_c_hbm, out_lat_ref, out_lon_ref, out_cor_ref,
    win_f_ref, win_c_ref, sems,
):
    win_f_ref[...] = nn(att16_ref[...], proj_ref[...])
    unit_field, inverse = norm_parts(x_ref[...])
    win_c_ref[...] = norm_back(cot_normed_ref[...], gain_ref[...], unit_field, inverse)
    stores = [
        pltpu.make_async_copy(win_f_ref, win_f_hbm, sems.at[0]),
        pltpu.make_async_copy(win_c_ref, win_c_hbm, sems.at[1]),
    ]
    for store in stores:
        store.start()
    out_strips = {"lat": out_lat_ref, "lon": out_lon_ref, "cor": out_cor_ref}
    for at, count, source, level, line, start in all_pieces():
        if source != "own":
            for array, src in enumerate((win_f_ref, win_c_ref)):
                dst = strip_row(source, array, level, line, start)
                out_strips[source][dst : dst + count, :] = src[at : at + count, :]
    for store in stores:
        store.wait()


def halve_kernel(bit, keep_ref, recv_ref, keep_out_ref, send_out_ref):
    total = keep_ref[...] + recv_ref[...]
    inner = {"x_low": 4, "y_low": 1, "y_high": 1, "x_high": 1}[bit]
    total = total.reshape(-1, 2, inner, *total.shape[1:])
    low, high = (total[:, i].reshape(keep_out_ref.shape) for i in range(2))
    own = {"x_low": lambda: lat_bit(3), "y_low": lambda: lat_bit(1), "y_high": lambda: lat_bit(2),
           "x_high": lambda: lax.axis_index("lon") // 8}[bit]()
    keep_out_ref[...] = jnp.where(own == 0, low, high)
    send_out_ref[...] = jnp.where(own == 0, high, low)


def xy_join_kernel(keep_ref, recv_ref, out_ref):
    out_ref[...] = keep_ref[...] + recv_ref[...]


def z_join_kernel(bias_ref, recv_ref, parts_ref, ff_ref, ff_recv_ref, out_ref):
    weights = jnp.concatenate(
        [ff_ref[0] + ff_recv_ref[0], jnp.sum(parts_ref[...], 0), jnp.zeros((16, LANES), f32)], 0
    )
    out_ref[:, :64, :] = bias_ref[...] + recv_ref[...]
    out_ref[:, 64:, :] = weights.reshape(8, 16, LANES)


def total_kernel(in_ref, out_ref):
    out_ref[...] = jnp.broadcast_to(jnp.sum(in_ref[...], 0)[None], out_ref.shape)


def spread_kernel(in_ref, out_ref, bias_ref):
    weights = in_ref[:, 64:, :].reshape(128, LANES)
    out_ref[...] = jnp.broadcast_to(weights[None, : 3 * PART + 4], out_ref.shape)
    bias_ref[...] = in_ref[:, :64, :]


def bias_kernel(next_ref, before_ref, bias_ref):
    first = half_at(1) == 0
    after, before = (ref[...].reshape(512, LANES) for ref in (next_ref, before_ref))
    packed = jnp.concatenate([jnp.where(first, after, before), jnp.where(first, before, after)], 0)
    lane = lax.broadcasted_iota(jnp.int32, (STACK, LANES), 1)
    third = STACK // 3
    rest = packed[2 * STACK : 2 * STACK + third]
    zeros = jnp.zeros((CELLS, LANES), f32)
    for band in range(BANDS):
        for level in range(LEV):
            table = packed[band * STACK : (band + 1) * STACK]
            if level == 1:
                table = pltpu.roll(table, 64, 1)
            k = band * LEV + level
            tail = jnp.concatenate([pltpu.roll(rest, (64 - g * 32 - k * 8) % LANES, 1) for g in range(3)], 0)
            table = jnp.where(lane < 64, table, jnp.where(lane < CELLS, tail, 0.0))
            for h in range(HEADS):
                rows = jnp.concatenate([table[h * CELLS : (h + 1) * CELLS], zeros], 1)
                if level == 1:
                    rows = pltpu.roll(rows, CELLS, 1)
                bias_ref[band, 0, h, level * CELLS : (level + 1) * CELLS, :] = rows[:, : 2 * CELLS]


def last_kernel(
    mine_ref, other_ref,
    gain_attn_ref, qkv_ref, proj_ref, gain_mlp_ref, up_ref, down_ref, rows_ref,
):
    gains = mine_ref[0, 3 * PART :, :]
    gains = jnp.concatenate([gains[:2], gains[2:4, :64]], 1)
    gain_mlp_ref[...] = gains[0:1]
    gain_attn_ref[...] = gains[1:2]
    own = lat_bit(0) == 0

    def tiles_of(k):
        found = []
        for low in (True, False):
            for j in range(CHIPS):
                mine, other = (ref[j, k * PART : (k + 1) * PART, :] for ref in (mine_ref, other_ref))
                rows_ref[j * PART : (j + 1) * PART, :] = jnp.where(own, mine, other) if low else jnp.where(own, other, mine)
            found += [rows_ref[t * D : (t + 1) * D, :] for t in range(3)]
        return found

    tiles = tiles_of(2)
    parts = [
        jnp.concatenate([tiles[i], tiles[4 + i // 2][:, 64 * (i % 2) : 64 * (i % 2) + 64]], 1)
        for i in range(4)
    ]
    qkv_ref[...] = jnp.concatenate(parts[:3], 1)
    proj_ref[...] = parts[3]
    up_ref[...] = jnp.concatenate(tiles_of(0), 1)
    down_ref[...] = jnp.concatenate(tiles_of(1), 1)


def stream_kernel(
    first_ref, cot_second_ref, win_f_hbm, win_c_hbm, lat_ref, lon_ref, cor_ref,
    in_first_ref, grad_second_ref, cot_ref, win_f_ref, win_c_ref, sems,
):
    loads = [
        pltpu.make_async_copy(win_f_hbm, win_f_ref, sems.at[0]),
        pltpu.make_async_copy(win_c_hbm, win_c_ref, sems.at[1]),
    ]
    for load in loads:
        load.start()
    cot_ref[...] = cot_second_ref[...].astype(f32)
    strips = {"lat": lat_ref, "lon": lon_ref, "cor": cor_ref}
    for array, window_ref in enumerate((win_f_ref, win_c_ref)):
        loads[array].wait()
        for at, count, source, level, line, start in all_pieces():
            if source == "own":
                part = window_ref[at : at + count, :]
                row, col = line, start
            else:
                row = line + (0 if source == "lon" else KEEP_R)
                col = start + (0 if source == "lat" else KEEP_C)
                place = strip_row(source, array, level, line, start)
                part = strips[source][place : place + count, :]
            spot = (level, row, slice(col, col + count))
            if array == 0:
                in_first_ref[spot] = first_ref[spot] - part
            else:
                grad_second_ref[spot] = cot_ref[spot] + part


def kernel(fn, out_shape, scratch=(), name=None, flops=0, nbytes=0, in_hbm=(), out_hbm=()):
    def spec(far):
        return pl.BlockSpec(memory_space=pltpu.HBM if far else pltpu.VMEM)

    def in_specs(count):
        return [spec(i in in_hbm) for i in range(count)]

    def call(*args):
        args = [
            pltpu.with_memory_space_constraint(x, pltpu.HBM) if i in in_hbm else x
            for i, x in enumerate(args)
        ]
        return pl.pallas_call(
            fn,
            out_shape=[s if hasattr(s, "dtype") else jax.ShapeDtypeStruct(s, f32) for s in out_shape],
            in_specs=in_specs(len(args)),
            out_specs=[spec(i in out_hbm) for i in range(len(out_shape))],
            scratch_shapes=[s if not isinstance(s, tuple) else pltpu.VMEM(*s) for s in scratch],
            compiler_params=pltpu.CompilerParams(vmem_limit_bytes=32 * 1024 * 1024),
            cost_estimate=pl.CostEstimate(flops=flops, bytes_accessed=nbytes, transcendentals=0),
            name=name,
        )(*args)

    return call


def body(
    out_first, out_second, cot_first, cot_second,
    gain_attn, w_qkv, w_proj, earth_bias, gain_mlp, w_up, w_down,
):
    lat_count, lon_count = lax.axis_size("lat"), lax.axis_size("lon")
    both = ("lat", "lon")
    shape = (LEV, ROWS, COLS, D)

    def halo(lat, lon, cor, by):
        ring = lambda n: [(i, (i + by) % n) for i in range(n)]
        diagonal = [
            (a * lon_count + o, ((a + by) % lat_count) * lon_count + (o + by) % lon_count)
            for a in range(lat_count)
            for o in range(lon_count)
        ]
        return (
            lax.ppermute(lat, "lat", ring(lat_count)),
            lax.ppermute(lon, "lon", ring(lon_count)),
            lax.ppermute(cor, both, diagonal),
        )

    same_z = [
        [(2 * chip + core) * lon_count + x * 8 + z for x in range(2) for chip in range(8)]
        for core in range(2)
        for z in range(8)
    ]
    same_x = [list(range(8)), list(range(8, 16))]

    def swap_xy(value):
        return lax.all_to_all(value, both, 0, 0, tiled=True, axis_index_groups=same_z)

    def swap_z(value):
        return lax.all_to_all(value, "lon", 0, 0, tiled=True, axis_index_groups=same_x)

    def across_x(value):
        return lax.ppermute(value, "lon", [(i, i ^ 8) for i in range(lon_count)])

    def along_x(value, by):
        def there(a, o):
            x = (o // 8 * 2 + a // 8 + by) % 4
            return (x % 2 * 8 + a % 8) * lon_count + x // 2 * 8 + o % 8

        pairs = [(a * lon_count + o, there(a, o)) for a in range(lat_count) for o in range(lon_count)]
        return lax.ppermute(value, both, pairs)

    def across(value, bit):
        return lax.ppermute(value, "lat", [(i, i ^ (1 << bit)) for i in range(lat_count)])

    strip_shapes = [(LAT_ROWS, D), (LON_ROWS, D), (COR_ROWS, D)]
    win = (TOKENS, D)
    ff_half = (CHIPS, 2 * PART, LANES)
    half_bytes = lambda *dims: jax.ShapeDtypeStruct(dims, bf16)
    (
        in_second, grad_first, x_win, g_win, lat, lon, cor, gain_mlp_part, hidden, cot_up, normed, cot,
    ) = kernel(
        ff_kernel,
        [
            shape, shape, win, win, *strip_shapes, (1, D),
            half_bytes(TOKENS, FF), half_bytes(TOKENS, FF), half_bytes(TOKENS, D), half_bytes(TOKENS, D),
        ],
        [
            (shape, f32), (shape, f32), (shape, bf16), (shape, bf16), ((D, FF), bf16), ((D, FF), bf16),
            (shape, f32), (shape, f32), ((1, D), f32),
            pltpu.SemaphoreType.DMA((7,)), pltpu.SemaphoreType.DMA((2,)),
        ],
        "feedforward",
        flops=8 * TOKENS * D * FF,
        nbytes=6_000_000,
        in_hbm=tuple(range(7)),
        out_hbm=(0, 1),
    )(out_first, out_second, cot_first, cot_second, gain_mlp.reshape(1, D), w_up, w_down.T)
    lat, lon, cor = halo(lat, lon, cor, 1)
    ff_keep, ff_send = kernel(
        ff_grads_kernel, [ff_half, ff_half], name="ffgrads", flops=2_000_000_000, nbytes=4_000_000
    )(normed, cot_up, cot, hidden)
    def ff_step(bit, keep, recv):
        parts = (keep.shape[0] // 2, *keep.shape[1:])
        return kernel(functools.partial(halve_kernel, bit), [parts, parts], name="halve")(keep, recv)

    ff_keep, ff_send = ff_step("x_low", ff_keep, across(ff_send, 0))
    x_inner = x_win
    x_win, ff_keep, ff_send = lax.optimization_barrier((x_win, ff_keep, ff_send))
    ff_recv = across(ff_send, 3)
    at_half = (CHIPS, PART + 4, LANES)
    bias_half = (8, 64, LANES)
    gain = gain_attn.reshape(1, D)
    half_win = half_bytes(*win)
    one = (LEV * CELLS, D)
    inner = kernel(
        inner_attention_kernel,
        [one, one, one, one, (LEV, STACK, LANES)],
        [(one, f32)] * 4,
        "inner",
        flops=4_000_000_000,
        nbytes=3_000_000,
    )(x_inner, g_win, earth_bias, gain, w_qkv, w_proj)
    bias_keep, bias_send, x_win, *attention_parts = kernel(
        attention_kernel,
        [bias_half, bias_half, win, *[half_win] * 6],
        [(win, f32)] * 9,
        "attention",
        flops=14_000_000_000,
        nbytes=16_000_000,
    )(x_win, g_win, lat, lon, cor, earth_bias, gain, w_qkv, w_proj, *inner)
    bias_keep, bias_recv = along_x(bias_keep, 1), along_x(bias_send, -1)
    keep, send, cot_normed = kernel(
        attention_grads_kernel, [at_half, at_half, win], name="attngrads", flops=2_000_000_000, nbytes=4_000_000
    )(x_win, *attention_parts, w_qkv, gain_mlp_part)
    attended = attention_parts[2]
    keep, send, x_win, ff_recv = lax.optimization_barrier((keep, send, x_win, ff_recv))
    ff_keep, ff_send = ff_step("y_low", ff_keep, ff_recv)
    ff_keep, ff_send = ff_step("y_high", ff_keep, across(ff_send, 1))
    ff_recv = across(ff_send, 2)
    win_f, win_c, lat, lon, cor = kernel(
        return_kernel,
        [win, win, *strip_shapes],
        [(win, f32), (win, f32), pltpu.SemaphoreType.DMA((2,))],
        "returns",
        flops=1_000_000_000,
        nbytes=4_000_000,
        out_hbm=(0, 1),
    )(x_win, attended, cot_normed, gain, w_proj)
    recv, win_f, win_c, lat, lon, cor = lax.optimization_barrier(
        (across(send, 0), win_f, win_c, lat, lon, cor)
    )
    lat, lon, cor = halo(lat, lon, cor, -1)
    block = (CHIPS, 3 * PART + 4, LANES)
    (parts,) = kernel(xy_join_kernel, [at_half], name="xyjoin")(keep, recv)
    parts, bias_keep, bias_recv, ff_recv = lax.optimization_barrier((parts, bias_keep, bias_recv, ff_recv))
    ff_keep, ff_send = ff_step("x_high", ff_keep, ff_recv)
    ff_recv = across_x(ff_send)
    parts = swap_xy(parts)
    (joined,) = kernel(z_join_kernel, [(8, 80, LANES)], name="zjoin")(
        bias_keep, bias_recv, parts, ff_keep, ff_recv
    )
    joined = swap_z(joined)
    (totals,) = kernel(total_kernel, [(8, 80, LANES)], name="total")(joined)
    totals = swap_z(totals)
    spread, bias_mine = kernel(spread_kernel, [block, bias_half], name="spread")(totals)
    bias_mine, bias_other = along_x(bias_mine, -1), along_x(bias_mine, 1)
    mine = swap_xy(spread)
    mine, lat, lon, cor = lax.optimization_barrier((mine, lat, lon, cor))
    in_first, grad_second = kernel(
        stream_kernel,
        [shape, shape],
        [(shape, f32), (win, f32), (win, f32), pltpu.SemaphoreType.DMA((2,))],
        "streams",
        nbytes=3_000_000,
        flops=2_000_000_000,
        in_hbm=(2, 3),
    )(out_first, cot_second, win_f, win_c, lat, lon, cor)
    mine, bias_mine, bias_other = lax.optimization_barrier((mine, bias_mine, bias_other))
    other = across(mine, 0)
    (grad_bias,) = kernel(bias_kernel, [(BANDS, 1, HEADS, 2 * CELLS, 2 * CELLS)], name="bias")(
        bias_mine, bias_other
    )
    grad_gain_attn, grad_qkv, grad_proj, grad_gain_mlp, grad_up, grad_down = kernel(
        last_kernel,
        [(1, D), (D, 3 * D), (D, D), (1, D), (D, FF), (D, FF)],
        [((3 * D, LANES), f32)],
        name="last",
        nbytes=6_000_000,
    )(mine, other)
    return (
        in_first, in_second, grad_first, grad_second,
        grad_gain_attn.reshape(D), grad_qkv, grad_proj, grad_bias,
        grad_gain_mlp.reshape(D), grad_up, grad_down.T,
    )


def solution(mesh):
    field = P(None, "lat", "lon", None)
    placed = (field,) * 4 + (P(), P(), P(), P("lat", None, None, None, None), P(), P(), P())
    return jax.shard_map(body, mesh=mesh, in_specs=placed, out_specs=placed, check_vma=False)
```

```python
import functools

import jax
import jax.numpy as jnp
from jax import lax
from jax.experimental import pallas as pl
from jax.experimental.pallas import tpu as pltpu
from jax.sharding import PartitionSpec as P

HEADS = 6
HEAD_DIM = 32
D = 192
FF = 768
LEV = 2
WIN_LAT = 6
WIN_LON = 12
CELLS = WIN_LAT * WIN_LON
BANDS = 2
CHIPS = 16
PART = 3 * 192 // 16
SECTORS = 2
ROWS = BANDS * WIN_LAT
COLS = SECTORS * WIN_LON
TOKENS = LEV * ROWS * COLS
HALF_LAT = WIN_LAT // 2
HALF_LON = WIN_LON // 2
STACK = HEADS * CELLS
LANES = 128

norm_eps = 1e-05
gelu_scale = 0.7978845608028654
gelu_cubic = 0.044715
masked_score = -1000000000.0
padded_score = -1e30
score_scale = HEAD_DIM ** (-0.5)

f32 = jnp.float32
bf16 = jnp.bfloat16


def nn(a, b):
    return lax.dot_general(a, b, (((1,), (0,)), ((), ())), preferred_element_type=f32)


def nt(a, b):
    return lax.dot_general(a, b, (((1,), (1,)), ((), ())), preferred_element_type=f32)


def tn(a, b):
    return lax.dot_general(a, b, (((0,), (0,)), ((), ())), preferred_element_type=f32)


def norm_parts(field):
    average = jnp.mean(field, -1, keepdims=True)
    centred = field - average
    inverse = lax.rsqrt(jnp.mean(centred * centred, -1, keepdims=True) + norm_eps)
    return (centred * inverse, inverse)


def norm_back(cot_normed, norm_gain, unit_field, inverse):
    cot_unit = cot_normed * norm_gain
    return inverse * (
        cot_unit
        - jnp.mean(cot_unit, -1, keepdims=True)
        - unit_field * jnp.mean(cot_unit * unit_field, -1, keepdims=True)
    )


def half_at(by):
    x = lax.axis_index("lon") // 8 * 2 + lax.axis_index("lat") // 8
    return lax.rem(x + by, 4) // 2


def lat_bit(k):
    return lax.rem(lax.axis_index("lat") // (1 << k), 2)


def lat_row(array, level, row):
    return ((array * LEV + level) * HALF_LAT + row) * (COLS - HALF_LON)


def lon_row(array, level, row):
    return ((array * LEV + level) * (ROWS - HALF_LAT) + row) * HALF_LON


def cor_row(array, level, row):
    return ((array * LEV + level) * HALF_LAT + row) * HALF_LON


LAT_ROWS = lat_row(2, 0, 0)
LON_ROWS = lon_row(2, 0, 0)
COR_ROWS = cor_row(2, 0, 0)
KEEP_R = ROWS - HALF_LAT
KEEP_C = COLS - HALF_LON


def ff_kernel(
    first_hbm, second_hbm, cot_first_hbm, cot_second_hbm, gain_hbm, up_hbm, down_hbm,
    in_second_hbm, grad_first_hbm, x_ref, g_ref, lat_ref, lon_ref, cor_ref, gain_out_ref,
    hidden_ref, cot_up_ref, normed_ref, cot_ref,
    first_ref, second_ref, cot_first_ref, cot_second_ref, up_ref, down_ref,
    in_second_ref, grad_first_ref, gain_ref, in_sems, out_sems,
):
    sources = (first_hbm, up_hbm, cot_second_hbm, down_hbm, second_hbm, cot_first_hbm, gain_hbm)
    targets = (first_ref, up_ref, cot_second_ref, down_ref, second_ref, cot_first_ref, gain_ref)
    loads = [pltpu.make_async_copy(x, y, in_sems.at[i]) for i, (x, y) in enumerate(zip(sources, targets))]
    for load in loads:
        load.start()
    loads[0].wait()
    loads[6].wait()
    tokens = first_ref[...].reshape(TOKENS, D)
    gain = gain_ref[...]
    unit_field, inverse = norm_parts(tokens)
    normed_ref[...] = (unit_field * gain).astype(bf16)
    for load in loads[1:4]:
        load.wait()
    cot = cot_second_ref[...].astype(f32).reshape(TOKENS, D).astype(bf16)
    cot_ref[...] = cot
    w_up = up_ref[...]
    w_down_t = down_ref[...]
    step = 96
    for i in range(TOKENS // step):
        part = pl.ds(i * step, step)
        up_proj = nn(normed_ref[part, :], w_up)
        square = up_proj * up_proj
        half = 0.5 * (1.0 + jnp.tanh(up_proj * (gelu_scale + gelu_scale * gelu_cubic * square)))
        hidden_ref[part, :] = (up_proj * half).astype(bf16)
        cot_hidden = nn(cot[i * step : (i + 1) * step], w_down_t)
        slope = half + (half * (1.0 - half)) * up_proj * (
            2.0 * gelu_scale + 6.0 * gelu_scale * gelu_cubic * square
        )
        cot_up_ref[part, :] = (cot_hidden * slope).astype(bf16)
    hidden = hidden_ref[...]
    cot_up = cot_up_ref[...]
    shape = (LEV, ROWS, COLS, D)
    loads[4].wait()
    in_second_ref[...] = second_ref[...] - nt(hidden, w_down_t).reshape(shape)
    stores = [
        pltpu.make_async_copy(in_second_ref, in_second_hbm, out_sems.at[0]),
        pltpu.make_async_copy(grad_first_ref, grad_first_hbm, out_sems.at[1]),
    ]
    stores[0].start()
    cot_normed = nt(cot_up, w_up)
    gain_out_ref[...] = jnp.sum(cot_normed * unit_field, 0, keepdims=True)
    back = norm_back(cot_normed, gain, unit_field, inverse)
    loads[5].wait()
    grad_first_ref[...] = cot_first_ref[...].astype(f32) + back.reshape(shape)
    stores[1].start()
    for array, ref in enumerate((in_second_ref, grad_first_ref)):
        for level in range(LEV):
            for row in range(HALF_LAT):
                at = lat_row(array, level, row)
                lat_ref[at : at + KEEP_C, :] = ref[level, KEEP_R + row, 0:KEEP_C, :]
                at = cor_row(array, level, row)
                cor_ref[at : at + HALF_LON, :] = ref[level, KEEP_R + row, KEEP_C:COLS, :]
            for row in range(KEEP_R):
                at = lon_row(array, level, row)
                lon_ref[at : at + HALF_LON, :] = ref[level, row, KEEP_C:COLS, :]
    for at, count, source, level, line, start in all_pieces():
        if source == "own":
            x_ref[at : at + count, :] = in_second_ref[level, line, start : start + count, :]
            g_ref[at : at + count, :] = grad_first_ref[level, line, start : start + count, :]
    for store in stores:
        store.wait()


def ff_grads_kernel(normed_ref, cot_up_ref, cot_ref, hidden_ref, keep_ref, send_ref):
    grad_up = tn(normed_ref[...], cot_up_ref[...])
    grad_down = tn(cot_ref[...], hidden_ref[...])
    for k, grad in enumerate((grad_up, grad_down)):
        tiles = [grad[:, t * LANES : (t + 1) * LANES] for t in range(6)]
        halves = [jnp.concatenate(tiles[3 * h : 3 * h + 3], 0) for h in range(2)]
        mine = lat_bit(0) == 0
        kept = jnp.where(mine, halves[0], halves[1])
        sent = jnp.where(mine, halves[1], halves[0])
        for j in range(CHIPS):
            keep_ref[j, k * PART : (k + 1) * PART, :] = kept[j * PART : (j + 1) * PART]
            send_ref[j, k * PART : (k + 1) * PART, :] = sent[j * PART : (j + 1) * PART]


def window_of(band, level, sector):
    return (band * LEV + level) * SECTORS + sector


def pieces(band, sector):
    for row in range(WIN_LAT):
        rolled = band * WIN_LAT + row
        edge = rolled < HALF_LAT
        line = rolled if edge else rolled - HALF_LAT
        if sector == 0:
            yield row, 0, HALF_LON, "cor" if edge else "lon", line, 0
            yield row, HALF_LON, HALF_LON, "lat" if edge else "own", line, 0
        else:
            yield row, 0, WIN_LON, "lat" if edge else "own", line, HALF_LON


def strip_row(source, array, level, line, column):
    place = {"lat": lat_row, "lon": lon_row, "cor": cor_row}[source]
    return place(array, level, line) + column


def all_pieces():
    for band in range(BANDS):
        for level in range(LEV):
            initial = (level - LEV // 2) % LEV
            for sector in range(SECTORS):
                base = window_of(band, level, sector) * CELLS
                for row, col, count, source, line, start in pieces(band, sector):
                    yield base + row * WIN_LON + col, count, source, initial, line, start


lane_head = lambda: lax.broadcasted_iota(jnp.int32, (CELLS, D), 1) // HEAD_DIM


def bias_table(bias_ref, band, level):
    query_low = lax.broadcasted_iota(jnp.int32, (CELLS, LANES), 0) < CELLS // 2
    key = lax.broadcasted_iota(jnp.int32, (CELLS, LANES), 1)
    first_band = lax.axis_index("lat") == 0
    apart = jnp.logical_and(query_low != (key < CELLS // 2), first_band)
    tables = []
    low = level * CELLS
    for h in range(HEADS):
        table = bias_ref[band, 0, h].astype(f32)[low : low + CELLS, low : low + CELLS]
        table = jnp.concatenate([table, jnp.full((CELLS, LANES - CELLS), padded_score, f32)], 1)
        if band == 0:
            table = jnp.where(jnp.logical_and(apart, key < CELLS), masked_score, table)
        tables.append(table)
    return jnp.concatenate(tables, 0)


def attend(query, key, value, cot_attended, table):
    heads = lane_head()
    of_head = [heads == h for h in range(HEADS)]
    pad = jnp.zeros((LANES - CELLS, D), f32)

    def stacked(value):
        return jnp.concatenate([jnp.where(m, value, 0.0) for m in of_head], 0).astype(bf16)

    def gathered(value):
        total = jnp.where(of_head[0], value[:CELLS], 0.0)
        for h in range(1, HEADS):
            total = jnp.where(of_head[h], value[h * CELLS : (h + 1) * CELLS], total)
        return total

    queries = stacked(query)
    key_part = jnp.concatenate([key, pad], 0).astype(bf16)
    value_part = jnp.concatenate([value, pad], 0).astype(bf16)
    scores = nt(queries, key_part) * score_scale + table
    exponent = jnp.exp(scores - jnp.max(scores, -1, keepdims=True))
    probability = exponent * (1.0 / jnp.sum(exponent, -1, keepdims=True))
    weights = probability.astype(bf16)
    attended = gathered(nn(weights, value_part))
    cot_att = stacked(cot_attended)
    cot_weights = nt(cot_att, value_part)
    cot_value = tn(weights, cot_att)[:CELLS]
    inner = jnp.sum(cot_weights * probability, -1, keepdims=True)
    cot_scores = probability * (cot_weights - inner)
    scaled = (cot_scores * score_scale).astype(bf16)
    cot_query = gathered(nn(scaled, key_part))
    cot_key = tn(scaled, queries)[:CELLS]
    return (attended, cot_query, cot_key, cot_value), cot_scores


def inner_attention_kernel(
    x_ref, g_ref, bias_ref, gain_ref, qkv_ref, proj_ref,
    att_ref, cq_ref, ck_ref, cv_ref, cot_scores_ref,
    q_ref, k_ref, v_ref, ca_ref,
):
    rows = [window_of(BANDS - 1, level, SECTORS - 1) * CELLS for level in range(LEV)]
    x, g = (jnp.concatenate([ref[at : at + CELLS, :] for at in rows], 0) for ref in (x_ref, g_ref))
    unit_field, _ = norm_parts(x)
    normed = (unit_field * gain_ref[...]).astype(bf16)
    for i, ref in enumerate((q_ref, k_ref, v_ref)):
        ref[...] = nn(normed, qkv_ref[:, i * D : (i + 1) * D]).astype(bf16).astype(f32)
    ca_ref[...] = nt(g.astype(bf16), proj_ref[...]).astype(bf16).astype(f32)
    for level in range(LEV):
        part = slice(level * CELLS, (level + 1) * CELLS)
        found, cot_scores = attend(
            q_ref[part, :], k_ref[part, :], v_ref[part, :], ca_ref[part, :],
            bias_table(bias_ref, BANDS - 1, level),
        )
        for ref, value in zip((att_ref, cq_ref, ck_ref, cv_ref), found):
            ref[part, :] = value
        cot_scores_ref[level] = cot_scores


def attention_kernel(
    x_in_ref, g_in_ref, lat_ref, lon_ref, cor_ref,
    bias_ref, gain_ref, qkv_ref, proj_ref,
    in_att_ref, in_cq_ref, in_ck_ref, in_cv_ref, in_cot_scores_ref,
    bias_keep_ref, bias_send_ref, x_ref, normed_ref, cot_low_ref, att16_ref, cq16_ref, ck16_ref, cv16_ref,
    g_ref, q_ref, k_ref, v_ref, ca_ref, att_ref, cq_ref, ck_ref, cv_ref,
):
    strips = {"lat": lat_ref, "lon": lon_ref, "cor": cor_ref}
    for at, count, source, level, line, start in all_pieces():
        for array, (dst, own) in enumerate(((x_ref, x_in_ref), (g_ref, g_in_ref))):
            if source == "own":
                dst[at : at + count, :] = own[at : at + count, :]
            else:
                src = strip_row(source, array, level, line, start)
                dst[at : at + count, :] = strips[source][src : src + count, :]
    unit_field, _ = norm_parts(x_ref[...])
    normed = (unit_field * gain_ref[...]).astype(bf16)
    for i, ref in enumerate((q_ref, k_ref, v_ref)):
        ref[...] = nn(normed, qkv_ref[:, i * D : (i + 1) * D]).astype(bf16).astype(f32)
    cot_low = g_ref[...].astype(bf16)
    ca_ref[...] = nt(cot_low, proj_ref[...]).astype(bf16).astype(f32)
    lane = lax.broadcasted_iota(jnp.int32, (STACK, LANES), 1)
    bias_grads = []
    for band in range(BANDS):
        for level in range(LEV):
            table = bias_table(bias_ref, band, level)
            bias_grad = None
            for sector in range(SECTORS):
                base = window_of(band, level, sector) * CELLS
                part = slice(base, base + CELLS)
                if band == BANDS - 1 and sector == SECTORS - 1:
                    given = slice(level * CELLS, (level + 1) * CELLS)
                    found = tuple(ref[given, :] for ref in (in_att_ref, in_cq_ref, in_ck_ref, in_cv_ref))
                    cot_scores = in_cot_scores_ref[level]
                else:
                    found, cot_scores = attend(
                        q_ref[part, :], k_ref[part, :], v_ref[part, :], ca_ref[part, :], table
                    )
                for ref, value in zip((att_ref, cq_ref, ck_ref, cv_ref), found):
                    ref[part, :] = value
                bias_grad = cot_scores if bias_grad is None else bias_grad + cot_scores
            bias_grads.append(bias_grad)
    left = [
        jnp.where(lane < 64, bias_grads[2 * b], pltpu.roll(bias_grads[2 * b + 1], 64, 1))
        for b in range(BANDS)
    ]
    lane3 = lane[: STACK // 3]
    rest = jnp.zeros((STACK // 3, LANES), f32)
    for g in range(3):
        for k in range(4):
            place = g * 32 + k * 8
            piece = bias_grads[k][g * (STACK // 3) : (g + 1) * (STACK // 3)]
            inside = jnp.logical_and(lane3 >= place, lane3 < place + 8)
            rest = jnp.where(inside, pltpu.roll(piece, (place - 64) % LANES, 1), rest)
    packed = jnp.concatenate([*left, rest, jnp.zeros((16, LANES), f32)], 0)
    packed = packed.reshape(2, 8, 64, LANES)
    for by, ref in ((1, bias_keep_ref), (3, bias_send_ref)):
        ref[...] = jnp.where(half_at(by) == 0, packed[0], packed[1])

    normed_ref[...] = normed
    cot_low_ref[...] = cot_low
    for src, dst in ((att_ref, att16_ref), (cq_ref, cq16_ref), (ck_ref, ck16_ref), (cv_ref, cv16_ref)):
        dst[...] = src[...].astype(bf16)


def attention_grads_kernel(
    x_ref, normed_ref, cot_low_ref, att16_ref, cq_ref, ck_ref, cv_ref, qkv_ref, gain_mlp_ref,
    keep_ref, send_ref, cot_normed_ref,
):
    unit_field, _ = norm_parts(x_ref[...])
    normed = normed_ref[...]
    grads = []
    cot_normed = None
    for i, ref in enumerate((cq_ref, ck_ref, cv_ref)):
        weight = qkv_ref[:, i * D : (i + 1) * D]
        cot_part = ref[...]
        grads.append(tn(normed, cot_part))
        term = nt(cot_part, weight)
        cot_normed = term if cot_normed is None else cot_normed + term
    grads.append(tn(att16_ref[...], cot_low_ref[...]))
    gain_part = jnp.sum(cot_normed * unit_field, 0, keepdims=True)
    cot_normed_ref[...] = cot_normed
    tiles = [g[:, :LANES] for g in grads]
    tiles += [jnp.concatenate([grads[i][:, LANES:], grads[i + 1][:, LANES:]], 1) for i in (0, 2)]
    halves = [jnp.concatenate(tiles[3 * h : 3 * h + 3], 0) for h in range(2)]
    mine = lat_bit(0) == 0
    kept = jnp.where(mine, halves[0], halves[1])
    sent = jnp.where(mine, halves[1], halves[0])
    gains = jnp.concatenate([gain_mlp_ref[...], gain_part], 0)
    right = jnp.concatenate([gains[:, LANES:], jnp.zeros((2, LANES - 64), f32)], 1)
    block = jnp.concatenate([gains[:, :LANES], right], 0)
    for ref, half in ((keep_ref, kept), (send_ref, sent)):
        for j in range(CHIPS):
            ref[j, :PART, :] = half[j * PART : (j + 1) * PART]
            ref[j, PART:, :] = block


def return_kernel(
    x_ref, att16_ref, cot_normed_ref, gain_ref, proj_ref,
    win_f_hbm, win_c_hbm, out_lat_ref, out_lon_ref, out_cor_ref,
    win_f_ref, win_c_ref, sems,
):
    win_f_ref[...] = nn(att16_ref[...], proj_ref[...])
    unit_field, inverse = norm_parts(x_ref[...])
    win_c_ref[...] = norm_back(cot_normed_ref[...], gain_ref[...], unit_field, inverse)
    stores = [
        pltpu.make_async_copy(win_f_ref, win_f_hbm, sems.at[0]),
        pltpu.make_async_copy(win_c_ref, win_c_hbm, sems.at[1]),
    ]
    for store in stores:
        store.start()
    out_strips = {"lat": out_lat_ref, "lon": out_lon_ref, "cor": out_cor_ref}
    for at, count, source, level, line, start in all_pieces():
        if source != "own":
            for array, src in enumerate((win_f_ref, win_c_ref)):
                dst = strip_row(source, array, level, line, start)
                out_strips[source][dst : dst + count, :] = src[at : at + count, :]
    for store in stores:
        store.wait()


def halve_kernel(bit, keep_ref, recv_ref, keep_out_ref, send_out_ref):
    total = keep_ref[...] + recv_ref[...]
    inner = {"x_low": 4, "y_low": 1, "y_high": 1, "x_high": 1}[bit]
    total = total.reshape(-1, 2, inner, *total.shape[1:])
    low, high = (total[:, i].reshape(keep_out_ref.shape) for i in range(2))
    own = {"x_low": lambda: lat_bit(3), "y_low": lambda: lat_bit(1), "y_high": lambda: lat_bit(2),
           "x_high": lambda: lax.axis_index("lon") // 8}[bit]()
    keep_out_ref[...] = jnp.where(own == 0, low, high)
    send_out_ref[...] = jnp.where(own == 0, high, low)


def xy_join_kernel(keep_ref, recv_ref, out_ref):
    out_ref[...] = keep_ref[...] + recv_ref[...]


def z_join_kernel(bias_ref, recv_ref, parts_ref, ff_ref, ff_recv_ref, out_ref):
    weights = jnp.concatenate(
        [ff_ref[0] + ff_recv_ref[0], jnp.sum(parts_ref[...], 0), jnp.zeros((16, LANES), f32)], 0
    )
    out_ref[:, :64, :] = bias_ref[...] + recv_ref[...]
    out_ref[:, 64:, :] = weights.reshape(8, 16, LANES)


def total_kernel(in_ref, out_ref):
    out_ref[...] = jnp.broadcast_to(jnp.sum(in_ref[...], 0)[None], out_ref.shape)


def spread_kernel(in_ref, out_ref, bias_ref):
    weights = in_ref[:, 64:, :].reshape(128, LANES)
    out_ref[...] = jnp.broadcast_to(weights[None, : 3 * PART + 4], out_ref.shape)
    bias_ref[...] = in_ref[:, :64, :]


def write_bias(next_ref, before_ref, bias_ref):
    first = half_at(1) == 0
    after, before = (ref[...].reshape(512, LANES) for ref in (next_ref, before_ref))
    packed = jnp.concatenate([jnp.where(first, after, before), jnp.where(first, before, after)], 0)
    lane = lax.broadcasted_iota(jnp.int32, (STACK, LANES), 1)
    third = STACK // 3
    rest = packed[2 * STACK : 2 * STACK + third]
    zeros = jnp.zeros((CELLS, LANES), f32)
    for band in range(BANDS):
        for level in range(LEV):
            table = packed[band * STACK : (band + 1) * STACK]
            if level == 1:
                table = pltpu.roll(table, 64, 1)
            k = band * LEV + level
            tail = jnp.concatenate([pltpu.roll(rest, (64 - g * 32 - k * 8) % LANES, 1) for g in range(3)], 0)
            table = jnp.where(lane < 64, table, jnp.where(lane < CELLS, tail, 0.0))
            for h in range(HEADS):
                rows = jnp.concatenate([table[h * CELLS : (h + 1) * CELLS], zeros], 1)
                if level == 1:
                    rows = pltpu.roll(rows, CELLS, 1)
                bias_ref[band, 0, h, level * CELLS : (level + 1) * CELLS, :] = rows[:, : 2 * CELLS]


def last_kernel(
    mine_ref, other_ref,
    gain_attn_ref, qkv_ref, proj_ref, gain_mlp_ref, up_ref, down_ref, rows_ref,
):
    gains = mine_ref[0, 3 * PART :, :]
    gains = jnp.concatenate([gains[:2], gains[2:4, :64]], 1)
    gain_mlp_ref[...] = gains[0:1]
    gain_attn_ref[...] = gains[1:2]
    own = lat_bit(0) == 0

    def tiles_of(k):
        found = []
        for low in (True, False):
            for j in range(CHIPS):
                mine, other = (ref[j, k * PART : (k + 1) * PART, :] for ref in (mine_ref, other_ref))
                rows_ref[j * PART : (j + 1) * PART, :] = jnp.where(own, mine, other) if low else jnp.where(own, other, mine)
            found += [rows_ref[t * D : (t + 1) * D, :] for t in range(3)]
        return found

    tiles = tiles_of(2)
    parts = [
        jnp.concatenate([tiles[i], tiles[4 + i // 2][:, 64 * (i % 2) : 64 * (i % 2) + 64]], 1)
        for i in range(4)
    ]
    qkv_ref[...] = jnp.concatenate(parts[:3], 1)
    proj_ref[...] = parts[3]
    up_ref[...] = jnp.concatenate(tiles_of(0), 1)
    down_ref[...] = jnp.concatenate(tiles_of(1), 1)


def stream_kernel(
    first_ref, cot_second_ref, win_f_hbm, win_c_hbm, lat_ref, lon_ref, cor_ref, bias_next_ref, bias_before_ref,
    in_first_ref, grad_second_ref, bias_ref, cot_ref, win_f_ref, win_c_ref, sems,
):
    loads = [
        pltpu.make_async_copy(win_f_hbm, win_f_ref, sems.at[0]),
        pltpu.make_async_copy(win_c_hbm, win_c_ref, sems.at[1]),
    ]
    for load in loads:
        load.start()
    write_bias(bias_next_ref, bias_before_ref, bias_ref)
    cot_ref[...] = cot_second_ref[...].astype(f32)
    strips = {"lat": lat_ref, "lon": lon_ref, "cor": cor_ref}
    for array, window_ref in enumerate((win_f_ref, win_c_ref)):
        loads[array].wait()
        for at, count, source, level, line, start in all_pieces():
            if source == "own":
                part = window_ref[at : at + count, :]
                row, col = line, start
            else:
                row = line + (0 if source == "lon" else KEEP_R)
                col = start + (0 if source == "lat" else KEEP_C)
                place = strip_row(source, array, level, line, start)
                part = strips[source][place : place + count, :]
            spot = (level, row, slice(col, col + count))
            if array == 0:
                in_first_ref[spot] = first_ref[spot] - part
            else:
                grad_second_ref[spot] = cot_ref[spot] + part


def kernel(fn, out_shape, scratch=(), name=None, flops=0, nbytes=0, in_hbm=(), out_hbm=()):
    def spec(far):
        return pl.BlockSpec(memory_space=pltpu.HBM if far else pltpu.VMEM)

    def in_specs(count):
        return [spec(i in in_hbm) for i in range(count)]

    def call(*args):
        args = [
            pltpu.with_memory_space_constraint(x, pltpu.HBM) if i in in_hbm else x
            for i, x in enumerate(args)
        ]
        return pl.pallas_call(
            fn,
            out_shape=[s if hasattr(s, "dtype") else jax.ShapeDtypeStruct(s, f32) for s in out_shape],
            in_specs=in_specs(len(args)),
            out_specs=[spec(i in out_hbm) for i in range(len(out_shape))],
            scratch_shapes=[s if not isinstance(s, tuple) else pltpu.VMEM(*s) for s in scratch],
            compiler_params=pltpu.CompilerParams(vmem_limit_bytes=32 * 1024 * 1024),
            cost_estimate=pl.CostEstimate(flops=flops, bytes_accessed=nbytes, transcendentals=0),
            name=name,
        )(*args)

    return call


def body(
    out_first, out_second, cot_first, cot_second,
    gain_attn, w_qkv, w_proj, earth_bias, gain_mlp, w_up, w_down,
):
    lat_count, lon_count = lax.axis_size("lat"), lax.axis_size("lon")
    both = ("lat", "lon")
    shape = (LEV, ROWS, COLS, D)

    def halo(lat, lon, cor, by):
        ring = lambda n: [(i, (i + by) % n) for i in range(n)]
        diagonal = [
            (a * lon_count + o, ((a + by) % lat_count) * lon_count + (o + by) % lon_count)
            for a in range(lat_count)
            for o in range(lon_count)
        ]
        return (
            lax.ppermute(lat, "lat", ring(lat_count)),
            lax.ppermute(lon, "lon", ring(lon_count)),
            lax.ppermute(cor, both, diagonal),
        )

    same_z = [
        [(2 * chip + core) * lon_count + x * 8 + z for x in range(2) for chip in range(8)]
        for core in range(2)
        for z in range(8)
    ]
    same_x = [list(range(8)), list(range(8, 16))]

    def swap_xy(value):
        return lax.all_to_all(value, both, 0, 0, tiled=True, axis_index_groups=same_z)

    def swap_z(value):
        return lax.all_to_all(value, "lon", 0, 0, tiled=True, axis_index_groups=same_x)

    def across_x(value):
        return lax.ppermute(value, "lon", [(i, i ^ 8) for i in range(lon_count)])

    def along_x(value, by):
        def there(a, o):
            x = (o // 8 * 2 + a // 8 + by) % 4
            return (x % 2 * 8 + a % 8) * lon_count + x // 2 * 8 + o % 8

        pairs = [(a * lon_count + o, there(a, o)) for a in range(lat_count) for o in range(lon_count)]
        return lax.ppermute(value, both, pairs)

    def across(value, bit):
        return lax.ppermute(value, "lat", [(i, i ^ (1 << bit)) for i in range(lat_count)])

    strip_shapes = [(LAT_ROWS, D), (LON_ROWS, D), (COR_ROWS, D)]
    win = (TOKENS, D)
    ff_half = (CHIPS, 2 * PART, LANES)
    half_bytes = lambda *dims: jax.ShapeDtypeStruct(dims, bf16)
    (
        in_second, grad_first, x_win, g_win, lat, lon, cor, gain_mlp_part, hidden, cot_up, normed, cot,
    ) = kernel(
        ff_kernel,
        [
            shape, shape, win, win, *strip_shapes, (1, D),
            half_bytes(TOKENS, FF), half_bytes(TOKENS, FF), half_bytes(TOKENS, D), half_bytes(TOKENS, D),
        ],
        [
            (shape, f32), (shape, f32), (shape, bf16), (shape, bf16), ((D, FF), bf16), ((D, FF), bf16),
            (shape, f32), (shape, f32), ((1, D), f32),
            pltpu.SemaphoreType.DMA((7,)), pltpu.SemaphoreType.DMA((2,)),
        ],
        "feedforward",
        flops=8 * TOKENS * D * FF,
        nbytes=6_000_000,
        in_hbm=tuple(range(7)),
        out_hbm=(0, 1),
    )(out_first, out_second, cot_first, cot_second, gain_mlp.reshape(1, D), w_up, w_down.T)
    lat, lon, cor = halo(lat, lon, cor, 1)
    ff_keep, ff_send = kernel(
        ff_grads_kernel, [ff_half, ff_half], name="ffgrads", flops=2_000_000_000, nbytes=4_000_000
    )(normed, cot_up, cot, hidden)
    def ff_step(bit, keep, recv):
        parts = (keep.shape[0] // 2, *keep.shape[1:])
        return kernel(functools.partial(halve_kernel, bit), [parts, parts], name="halve")(keep, recv)

    ff_keep, ff_send = ff_step("x_low", ff_keep, across(ff_send, 0))
    x_inner = x_win
    x_win, ff_keep, ff_send = lax.optimization_barrier((x_win, ff_keep, ff_send))
    ff_recv = across(ff_send, 3)
    at_half = (CHIPS, PART + 4, LANES)
    bias_half = (8, 64, LANES)
    gain = gain_attn.reshape(1, D)
    half_win = half_bytes(*win)
    one = (LEV * CELLS, D)
    inner = kernel(
        inner_attention_kernel,
        [one, one, one, one, (LEV, STACK, LANES)],
        [(one, f32)] * 4,
        "inner",
        flops=4_000_000_000,
        nbytes=3_000_000,
    )(x_inner, g_win, earth_bias, gain, w_qkv, w_proj)
    bias_keep, bias_send, x_win, *attention_parts = kernel(
        attention_kernel,
        [bias_half, bias_half, win, *[half_win] * 6],
        [(win, f32)] * 9,
        "attention",
        flops=14_000_000_000,
        nbytes=16_000_000,
    )(x_win, g_win, lat, lon, cor, earth_bias, gain, w_qkv, w_proj, *inner)
    bias_keep, bias_recv = along_x(bias_keep, 1), along_x(bias_send, -1)
    keep, send, cot_normed = kernel(
        attention_grads_kernel, [at_half, at_half, win], name="attngrads", flops=2_000_000_000, nbytes=4_000_000
    )(x_win, *attention_parts, w_qkv, gain_mlp_part)
    attended = attention_parts[2]
    keep, send, x_win, ff_recv = lax.optimization_barrier((keep, send, x_win, ff_recv))
    ff_keep, ff_send = ff_step("y_low", ff_keep, ff_recv)
    ff_keep, ff_send = ff_step("y_high", ff_keep, across(ff_send, 1))
    ff_recv = across(ff_send, 2)
    win_f, win_c, lat, lon, cor = kernel(
        return_kernel,
        [win, win, *strip_shapes],
        [(win, f32), (win, f32), pltpu.SemaphoreType.DMA((2,))],
        "returns",
        flops=1_000_000_000,
        nbytes=4_000_000,
        out_hbm=(0, 1),
    )(x_win, attended, cot_normed, gain, w_proj)
    recv, win_f, win_c, lat, lon, cor = lax.optimization_barrier(
        (across(send, 0), win_f, win_c, lat, lon, cor)
    )
    lat, lon, cor = halo(lat, lon, cor, -1)
    block = (CHIPS, 3 * PART + 4, LANES)
    (parts,) = kernel(xy_join_kernel, [at_half], name="xyjoin")(keep, recv)
    parts, bias_keep, bias_recv, ff_recv = lax.optimization_barrier((parts, bias_keep, bias_recv, ff_recv))
    ff_keep, ff_send = ff_step("x_high", ff_keep, ff_recv)
    ff_recv = across_x(ff_send)
    parts = swap_xy(parts)
    (joined,) = kernel(z_join_kernel, [(8, 80, LANES)], name="zjoin")(
        bias_keep, bias_recv, parts, ff_keep, ff_recv
    )
    joined = swap_z(joined)
    (totals,) = kernel(total_kernel, [(8, 80, LANES)], name="total")(joined)
    totals = swap_z(totals)
    spread, bias_mine = kernel(spread_kernel, [block, bias_half], name="spread")(totals)
    bias_mine, bias_other = along_x(bias_mine, -1), along_x(bias_mine, 1)
    mine = swap_xy(spread)
    mine, lat, lon, cor = lax.optimization_barrier((mine, lat, lon, cor))
    mine, bias_mine, bias_other = lax.optimization_barrier((mine, bias_mine, bias_other))
    other = across(mine, 0)
    in_first, grad_second, grad_bias = kernel(
        stream_kernel,
        [shape, shape, (BANDS, 1, HEADS, 2 * CELLS, 2 * CELLS)],
        [(shape, f32), (win, f32), (win, f32), pltpu.SemaphoreType.DMA((2,))],
        "streams",
        nbytes=3_000_000,
        flops=2_000_000_000,
        in_hbm=(2, 3),
    )(out_first, cot_second, win_f, win_c, lat, lon, cor, bias_mine, bias_other)
    grad_gain_attn, grad_qkv, grad_proj, grad_gain_mlp, grad_up, grad_down = kernel(
        last_kernel,
        [(1, D), (D, 3 * D), (D, D), (1, D), (D, FF), (D, FF)],
        [((3 * D, LANES), f32)],
        name="last",
        nbytes=6_000_000,
    )(mine, other)
    return (
        in_first, in_second, grad_first, grad_second,
        grad_gain_attn.reshape(D), grad_qkv, grad_proj, grad_bias,
        grad_gain_mlp.reshape(D), grad_up, grad_down.T,
    )


def solution(mesh):
    field = P(None, "lat", "lon", None)
    placed = (field,) * 4 + (P(), P(), P(), P("lat", None, None, None, None), P(), P(), P())
    return jax.shard_map(body, mesh=mesh, in_specs=placed, out_specs=placed, check_vma=False)
```
